256 devices in a mesh: tm: 16 (over z, y_hi), space: 16 (over y_lo, x, core).
Axes of the slice: x: 4, y: 4 (y_hi: 2, y_lo: 2; y = y_hi * 2 + y_lo), z: 8, core: 2. Of those that a mesh axis runs over, the one named last changes fastest.
Arguments:
- forcing: float32 [32, 12, 32, 2048], P('tm', None, 'space'), may hold values from -8 to 8
- iterate: float32 [32, 12, 32, 2048], P('tm', None, 'space'), may hold values from -8 to 8
- initial_state: float32 [12, 32, 2048], P(None, 'space'), may hold values from -8 to 8
- damping: float32 [12, 32, 2048], P(None, 'space'), may hold values from 0.5 to 1.5
- mixing: float32 [12, 12], replicated, may hold values from -0.12 to 0.12, as said below
- stencil: float32 [26, 12], replicated, may hold values from 0 to 0.04
Outputs:
- updated: float32 [32, 12, 32, 2048], P('tm', None, 'space')
- defect_vector: float32 [32, 12, 32, 2048], P('tm', None, 'space')
The draws below stay inside these ranges and needn't reach their ends.
Inputs may be any that keep to these rules, and one draw needn't show every extreme that they name: `mixing`: the diagonal entries lie between 0 and 0.1; the others between -0.12 and 0.12.
All inputs are finite; a program needn't handle non-finite values.
Results may differ from the reference program's by a relative error of at most 0.0003.
Values sent between devices are 32-bit elements; how exact they have to be, the bound alone decides.
A program may use at most 64 MiB of HBM per device.

```python
import math
import jax
import jax.numpy as jnp
from jax import lax

C = 12
NZ = 64
SWEEPS = 2
HORIZON_COUNT = 32
NX = 32
PLANE = 2048


def draw_mixing(key, part):
    key = jax.random.fold_in(key, 7)
    coupling_key, diagonal_key = jax.random.split(key)
    coupling = jax.random.uniform(coupling_key, (C, C), jnp.float32, -0.12, 0.12)
    diagonal_values = jax.random.uniform(diagonal_key, (C,), jnp.float32, 0.0, 0.1)
    identity_mask = jnp.eye(C, dtype=jnp.float32)
    return coupling * (1.0 - identity_mask) + identity_mask * diagonal_values[None, :]


def block_scale(rng, shape, shards, smallest, high):
    def one(axis_at, parts):
        heights = jax.random.uniform(jax.random.fold_in(jax.random.fold_in(rng, 6), axis_at), (parts,), jnp.float32, smallest / len(shards), high / len(shards))
        return jnp.repeat(jnp.exp(heights), shape[axis_at] // parts).reshape((-1,) + (1,) * (len(shape) - axis_at - 1))

    factor_of = one(*shards[0])
    for cut in shards[1:]:
        factor_of = factor_of * one(*cut)
    return factor_of


def normal_values(own_key, shape, scale, reach, cuts=(), kind=jnp.bfloat16):
    level = block_scale(own_key, shape, cuts, -0.22, 0.18) if cuts else 1.0
    result = jax.random.normal(own_key, shape, jnp.float32) * scale * level
    return jnp.minimum(jnp.maximum(result, -reach), reach).astype(kind)


def setup_inputs(seed: int = 0) -> dict:
    key_list = jax.random.split(jax.random.key(seed), 7)
    forcing = normal_values(key_list[0], (HORIZON_COUNT, C, NX, PLANE), 1.0, 8.0, ((0, 16), (2, 16)), jnp.float32)
    iterate = normal_values(key_list[1], (HORIZON_COUNT, C, NX, PLANE), 1.0, 8.0, ((0, 16), (2, 16)), jnp.float32)
    initial_state = normal_values(key_list[2], (C, NX, PLANE), 1.0, 8.0, ((1, 16),), jnp.float32)
    damping = jnp.clip(0.5 + 1.0 * jax.random.uniform(key_list[3], (C, NX, PLANE), jnp.float32) ** block_scale(key_list[3], (C, NX, PLANE), ((1, 16),), -0.2, 0.2), 0.5, 1.5)
    mixing = draw_mixing(jax.random.fold_in(key_list[6], 71), 0)
    stencil = jnp.clip(jax.random.uniform(key_list[5], (26, C), jnp.float32, 0.0, 0.04), 0.0, 0.04)
    return {"forcing": forcing, "iterate": iterate, "initial_state": initial_state, "damping": damping, "mixing": mixing, "stencil": stencil}


wrap_weight = 0.05


def plane_shift(field, shift_y, shift_z):
    offset = shift_y * NZ + shift_z
    extent = field.shape[-1]
    if offset > 0:
        filler = jnp.zeros(field.shape[:-1] + (offset,), field.dtype)
        shifted = jnp.concatenate([field[..., offset:], filler], axis=-1)
    elif offset < 0:
        filler = jnp.zeros(field.shape[:-1] + (-offset,), field.dtype)
        shifted = jnp.concatenate([filler, field[..., :offset]], axis=-1)
    else:
        shifted = field
    if shift_z != 0:
        depth = jnp.arange(extent) % NZ + shift_z
        shifted = jnp.where((depth >= 0) & (depth < NZ), shifted, jnp.zeros_like(shifted))
    return shifted


def operate(padded, damping, mixing, stencil):
    extent = padded.shape[-2] - 2
    centre = padded[..., 1:1 + extent, :]
    applied = damping * centre + jnp.einsum("cd,...dxp->...cxp", mixing, centre, precision=lax.Precision.HIGHEST)
    counter = 0
    for offset_x in (-1, 0, 1):
        sheet = padded[..., 1 + offset_x:1 + offset_x + extent, :]
        for offset_y in (-1, 0, 1):
            for offset_z in (-1, 0, 1):
                if offset_x == 0 and offset_y == 0 and offset_z == 0:
                    continue
                applied = applied - stencil[counter][:, None, None] * plane_shift(sheet, offset_y, offset_z)
                counter += 1
    return applied


def divide(numer_re, numer_im, gain, real_shift, imag_shift):
    denom_re = real_shift + gain
    squared = denom_re ** 2 + imag_shift ** 2
    return (numer_re * denom_re + numer_im * imag_shift) / squared, (numer_im * denom_re - numer_re * imag_shift) / squared


def relax(padded, source, damping, gain, real_shift, imag_shift, mixing, stencil):
    extent = padded.shape[-2] - 2
    current = padded[..., 1:1 + extent, :]
    applied = operate(padded, damping, mixing, stencil)
    image_re = real_shift * current[0] - imag_shift * current[1] + applied[0]
    image_im = real_shift * current[1] + imag_shift * current[0] + applied[1]
    step_re, step_im = divide(source[0] - image_re, source[1] - image_im, gain, real_shift, imag_shift)
    return jnp.stack([current[0] + step_re, current[1] + step_im])


def reference(forcing, iterate, initial_state, damping, mixing, stencil):
    previous = jnp.concatenate([initial_state[None], iterate[:-1]], axis=0)
    padded = jnp.pad(iterate, ((0, 0), (0, 0), (1, 1), (0, 0)))
    defect_vector = forcing - (iterate - previous + operate(padded, damping, mixing, stencil))
    decay_coefficient = math.log(wrap_weight) / HORIZON_COUNT
    wrap_root = math.exp(decay_coefficient)
    moment_samples = jnp.arange(HORIZON_COUNT).astype(jnp.float32)
    circulant_factor_weighted = defect_vector * jnp.exp(decay_coefficient * moment_samples)[:, None, None, None]
    spectrum = jnp.fft.fft(circulant_factor_weighted, axis=0)
    spec_real = jnp.real(spectrum).astype(jnp.float32)
    spec_imag = jnp.imag(spectrum).astype(jnp.float32)
    gain = damping + jnp.diagonal(mixing)[:, None, None]

    def solve_one(inputs):
        source_re, source_im, frequency = inputs
        twiddle_phase_radians = (2.0 * math.pi / HORIZON_COUNT) * frequency
        real_shift = 1.0 - wrap_root * jnp.cos(twiddle_phase_radians)
        imag_shift = wrap_root * jnp.sin(twiddle_phase_radians)
        source = jnp.stack([source_re, source_im])
        current = jnp.stack(divide(source_re, source_im, gain, real_shift, imag_shift))
        for sweep_number in range(SWEEPS - 1):
            padded_current = jnp.pad(current, ((0, 0), (0, 0), (1, 1), (0, 0)))
            current = relax(padded_current, source, damping, gain, real_shift, imag_shift, mixing, stencil)
        return current

    solved = lax.map(solve_one, (spec_real, spec_imag, jnp.arange(HORIZON_COUNT).astype(jnp.float32)))
    retarded_offset_entry = jnp.real(jnp.fft.ifft(solved[:, 0] + 1j * solved[:, 1], axis=0)).astype(jnp.float32)
    horizon_update = retarded_offset_entry * jnp.exp(-decay_coefficient * moment_samples)[:, None, None, None]
    return iterate + horizon_update, defect_vector
```

```python
import functools

import jax
import jax.numpy as jnp
from jax import lax
from jax.experimental import pallas as pl
from jax.experimental.pallas import tpu as pltpu
from jax.sharding import PartitionSpec as P

NZ = 64
LANES = 128
wrap_weight = 0.05
MESH = pl.DeviceIdType.MESH
NG, GC = 3, 4


def kernel(
    f_ref, x_ref, init_ref, damp_ref, mix_ref, st_ref,
    upd_ref, def_ref,
    xb, xh, q, qh, ini, prev, a, ah, e, r, co, cc, ch, u, b, e2, r2, co2, c2,
    prev_sem, xh_send, xh_recv, qh_send, qh_recv, ah_send, ah_recv, ch_send, ch_recv,
    s_send, s_recv,
):
    groups = lax.axis_size("tm")
    t = lax.axis_index("tm")
    slabs = lax.axis_size("space")
    s = lax.axis_index("space")
    has_low, has_high = s > 0, s < slabs - 1

    barrier = pltpu.get_barrier_semaphore()
    for k in range(1, groups):
        pl.semaphore_signal(barrier, inc=1, device_id={"tm": lax.rem(t + k, groups)}, device_id_type=MESH)

    @pl.when(has_low)
    def _():
        pl.semaphore_signal(barrier, inc=1, device_id={"space": s - 1}, device_id_type=MESH)

    @pl.when(has_high)
    def _():
        pl.semaphore_signal(barrier, inc=1, device_id={"space": s + 1}, device_id_type=MESH)

    lane = lax.broadcasted_iota(jnp.int32, (16, LANES), 1)
    row = lax.broadcasted_iota(jnp.int32, (16, LANES), 0)
    depth = lane % NZ
    half = lane < NZ

    def plane(ref, *index):
        return ref[index].reshape(16, LANES)

    def z_shifts(p):
        before = jnp.where(depth == 0, 0.0, pltpu.roll(p, 1, 1))
        after = jnp.where(depth == NZ - 1, 0.0, pltpu.roll(p, LANES - 1, 1))
        return before, p, after

    def y_before(p):
        turned = pltpu.roll(p, NZ, 1)
        return jnp.where(half, jnp.where(row == 0, 0.0, pltpu.roll(turned, 1, 0)), turned)

    def y_after(p):
        turned = pltpu.roll(p, NZ, 1)
        return jnp.where(half, turned, jnp.where(row == 15, 0.0, pltpu.roll(turned, 15, 0)))

    def neighbours(sheets, channel):
        shifted = [z_shifts(p) for p in sheets]
        out = []
        for at in range(2):
            sums = []
            for oy in range(3):
                total = None
                for ox in range(3):
                    for oz in range(3):
                        place = ox * 9 + oy * 3 + oz
                        if place == 13:
                            continue
                        term = st_ref[place - (place > 13), channel] * shifted[at + ox][oz]
                        total = term if total is None else total + term
                sums.append(total)
            out.append(sums[1] + y_before(sums[0]) + y_after(sums[2]))
        return out

    def to_sides(buf, halo, send, recv, sem):
        def low():
            return pltpu.make_async_remote_copy(
                buf(0), halo(1), send.at[1, sem], recv.at[1, sem], device_id={"space": s - 1}, device_id_type=MESH
            )

        def high():
            return pltpu.make_async_remote_copy(
                buf(1), halo(0), send.at[0, sem], recv.at[0, sem], device_id={"space": s + 1}, device_id_type=MESH
            )

        def start():
            pl.when(has_low)(lambda: low().start())
            pl.when(has_high)(lambda: high().start())

        def wait_recv():
            pl.when(has_low)(lambda: high().wait_recv())
            pl.when(has_high)(lambda: low().wait_recv())

        def wait_send():
            pl.when(has_low)(lambda: low().wait_send())
            pl.when(has_high)(lambda: high().wait_send())

        return start, wait_recv, wait_send

    def x_sides(g):
        return to_sides(lambda x: xb.at[:, g, :, pl.ds(2 * x, 2)], lambda x: xh.at[x, :, g], xh_send, xh_recv, g)

    def q_sides():
        return to_sides(lambda x: q.at[:, :, pl.ds(2 * x, 2)], lambda x: qh.at[x], qh_send, qh_recv, 0)

    def a_sides(g):
        return to_sides(lambda x: a.at[:, g, :, pl.ds(2 * x, 2)], lambda x: ah.at[x, :, g], ah_send, ah_recv, g)

    def c_sides(g):
        return to_sides(lambda x: cc.at[g, :, pl.ds(2 * x, 2)], lambda x: ch.at[x, g], ch_send, ch_recv, g)

    def chunk(ref, g, owner):
        return ref.at[g, owner // 4, owner % 4]

    def gather(src, dst, stage, g):
        for k in range(1, groups):
            owner = lax.rem(t + k, groups)
            pltpu.make_async_remote_copy(
                chunk(src, g, owner), dst.at[g, t], s_send.at[stage, g], s_recv.at[stage, g],
                device_id={"tm": owner}, device_id_type=MESH,
            ).start()
        dst[g, t] = src[g, t // 4, t % 4]

    def scatter(src, dst, stage, g):
        for k in range(1, groups):
            to = lax.rem(t + k, groups)
            pltpu.make_async_remote_copy(
                src.at[g, to], chunk(dst, g, t), s_send.at[stage, g], s_recv.at[stage, g],
                device_id={"tm": to}, device_id_type=MESH,
            ).start()
        dst[g, t // 4, t % 4] = src[g, t]

    def await_all(stage, g, sem):
        some = r.at[g, pl.ds(0, groups - 1)]
        pltpu.make_async_copy(some, some, sem.at[stage, g]).wait()

    def solve(src, dst, g, first):
        rate = q[g, t // 4, t % 4]
        rate = rate * rate
        total, power = src[g, 0], rate
        for n in range(1, groups):
            total = rate * total + src[g, n]
            power = power * rate
        total = wrap_weight * total if first is None else first + wrap_weight * total
        carry = total / (1.0 - wrap_weight * power)
        for n in range(groups):
            dst[g, n] = carry
            if n < groups - 1:
                carry = rate * carry + src[g, n]

    def split(c, _):
        for n in range(2):
            for x in range(2):
                xb[n, c // GC, c % GC, pl.ds(2 * x, 2)] = x_ref[n, c, pl.ds(x, 16, 2), :].reshape(2, 8, LANES)
        return 0

    lax.fori_loop(0, NG * GC, split, 0)
    edges = has_low.astype(jnp.int32) + has_high.astype(jnp.int32)
    pl.semaphore_wait(barrier, groups - 1 + edges)

    for g in range(NG):
        x_sides(g)[0]()

    def previous():
        return pltpu.make_async_remote_copy(
            x_ref.at[1], prev, prev_sem.at[0], prev_sem.at[1], device_id={"tm": t + 1}, device_id_type=MESH
        )

    pl.when(t < groups - 1)(lambda: previous().start())

    def rates(c, _):
        g, i = c // GC, c % GC
        for x in range(2):
            gain = damp_ref[c, pl.ds(x, 16, 2), :] + mix_ref[c, c]
            q[g, i, pl.ds(2 * x, 2)] = (1.0 / (1.0 + gain)).reshape(2, 8, LANES)
            ini[g, i, pl.ds(2 * x, 2)] = init_ref[c, pl.ds(x, 16, 2), :].reshape(2, 8, LANES)
        return 0

    lax.fori_loop(0, NG * GC, rates, 0)
    q_sides()[0]()

    for side, exists in ((0, has_low), (1, has_high)):

        @pl.when(jnp.logical_not(exists))
        def _(side=side):
            xh[side] = jnp.zeros(xh.shape[1:], jnp.float32)
            qh[side] = jnp.zeros(qh.shape[1:], jnp.float32)
            ah[side] = jnp.zeros(ah.shape[1:], jnp.float32)
            ch[side] = jnp.zeros(ch.shape[1:], jnp.float32)

    keep = jnp.where(t < groups - 1, 1.0, 0.0)

    def defects(g, _):
        x_sides(g)[1]()

        def channel(i, _):
            c = g * GC + i
            parts = []
            for n in range(2):
                own = [plane(xb, n, g, i, pl.ds(2 * x, 2)) for x in range(2)]
                near = neighbours([plane(xh, 0, n, g, i), *own, plane(xh, 1, n, g, i)], c)
                for x in range(2):
                    applied = damp_ref[c, pl.ds(x, 16, 2), :] * own[x] - near[x]
                    for d in range(NG * GC):
                        applied = applied + mix_ref[c, d] * plane(xb, n, d // GC, d % GC, pl.ds(2 * x, 2))
                    parts.append((own[x], applied))
            for x in range(2):
                at = pl.ds(2 * x, 2)
                (x0, k0), (x1, k1) = parts[x], parts[2 + x]
                d0 = f_ref[0, c, pl.ds(x, 16, 2), :] - (x0 + k0)
                d1 = f_ref[1, c, pl.ds(x, 16, 2), :] - (x1 - x0 + k1)
                rate = plane(q, g, i, at)
                a0 = rate * d0
                a1 = rate * (a0 + d1)
                def_ref[0, c, pl.ds(x, 16, 2), :] = d0
                def_ref[1, c, pl.ds(x, 16, 2), :] = d1
                a[0, g, i, at] = a0.reshape(2, 8, LANES)
                a[1, g, i, at] = a1.reshape(2, 8, LANES)
                e[g, i, at] = (a1 + keep * x1).reshape(2, 8, LANES)
            return 0

        lax.fori_loop(0, GC, channel, 0)
        gather(e, r, 0, g)
        a_sides(g)[0]()
        return 0

    lax.fori_loop(0, NG, defects, 0)

    def carries(g, _):
        await_all(0, g, s_recv)
        solve(r, co, g, ini[g, t // 4, t % 4])
        scatter(co, cc, 1, g)
        return 0

    lax.fori_loop(0, NG, carries, 0)
    q_sides()[1]()

    def first_sweep(g, _):
        await_all(1, g, s_recv)
        c_sides(g)[0]()

        def channel(i, _):
            rate, carry = q[g, i], cc[g, i]
            moved = rate * carry
            u[0, g, i] = a[0, g, i] + moved
            u[1, g, i] = a[1, g, i] + rate * moved
            return 0

        lax.fori_loop(0, GC, channel, 0)
        return 0

    lax.fori_loop(0, NG, first_sweep, 0)

    def second_sweep(g, _):
        a_sides(g)[1]()
        c_sides(g)[1]()

        def channel(i, _):
            c = g * GC + i
            halos = []
            for side in range(2):
                rate = plane(qh, side, g, i)
                moved = rate * plane(ch, side, g, i)
                halos.append((plane(ah, side, 0, g, i) + moved, plane(ah, side, 1, g, i) + rate * moved))
            parts = []
            for n in range(2):
                own = [plane(u, n, g, i, pl.ds(2 * x, 2)) for x in range(2)]
                near = neighbours([halos[0][n], *own, halos[1][n]], c)
                for x in range(2):
                    value = near[x]
                    for d in range(NG * GC):
                        weight = jnp.where(c == d, 0.0, mix_ref[c, d])
                        value = value - weight * plane(u, n, d // GC, d % GC, pl.ds(2 * x, 2))
                    parts.append((own[x], value))
            for x in range(2):
                at = pl.ds(2 * x, 2)
                (u0, h0), (u1, h1) = parts[x], parts[2 + x]
                rate = plane(q, g, i, at)
                v0 = rate * h0
                v1 = rate * (v0 + h1)
                b[0, g, i, at] = (plane(xb, 0, g, i, at) + (u0 + v0)).reshape(2, 8, LANES)
                b[1, g, i, at] = (plane(xb, 1, g, i, at) + (u1 + v1)).reshape(2, 8, LANES)
                e2[g, i, at] = v1.reshape(2, 8, LANES)
            return 0

        lax.fori_loop(0, GC, channel, 0)
        gather(e2, r2, 2, g)
        return 0

    lax.fori_loop(0, NG, second_sweep, 0)

    def carries_2(g, _):
        await_all(2, g, s_recv)
        solve(r2, co2, g, None)
        scatter(co2, c2, 3, g)
        return 0

    lax.fori_loop(0, NG, carries_2, 0)

    @pl.when(t > 0)
    def _():
        previous().wait_recv()
        def_ref[0] = def_ref[0] + prev[...]

    @pl.when(t == 0)
    def _():
        def_ref[0] = def_ref[0] + init_ref[...]

    def finish(g, _):
        await_all(3, g, s_recv)

        def channel(i, _):
            for x in range(2):
                at = pl.ds(2 * x, 2)
                rate = plane(q, g, i, at)
                moved = rate * plane(c2, g, i, at)
                upd_ref[0, g * GC + i, pl.ds(x, 16, 2), :] = plane(b, 0, g, i, at) + moved
                upd_ref[1, g * GC + i, pl.ds(x, 16, 2), :] = plane(b, 1, g, i, at) + rate * moved
            return 0

        lax.fori_loop(0, GC, channel, 0)
        return 0

    lax.fori_loop(0, NG, finish, 0)

    pl.when(t < groups - 1)(lambda: previous().wait_send())
    q_sides()[2]()
    for g in range(NG):
        x_sides(g)[2]()
        a_sides(g)[2]()
        c_sides(g)[2]()
        for stage in range(4):
            await_all(stage, g, s_send)


def rows_of(value):
    lead = value.shape[:-2]
    value = value.reshape(lead + (2, 16, LANES))
    return jnp.swapaxes(value, -3, -2).reshape(lead + (32, LANES))


def planes_of(value):
    lead = value.shape[:-2]
    value = value.reshape(lead + (16, 2, LANES))
    return jnp.swapaxes(value, -3, -2).reshape(lead + (2, 16 * LANES))


def body(forcing, iterate, initial_state, damping, mixing, stencil):
    vmem = pl.BlockSpec(memory_space=pltpu.VMEM)
    smem = pl.BlockSpec(memory_space=pltpu.SMEM)

    def field(*lead):
        return pltpu.VMEM((*lead, NG, GC, 4, 8, LANES), jnp.float32)

    def face(*lead):
        return pltpu.VMEM((*lead, NG, GC, 2, 8, LANES), jnp.float32)

    slots = pltpu.VMEM((NG, 16, 8, LANES), jnp.float32)
    dma = pltpu.SemaphoreType.DMA
    updated, defect = pl.pallas_call(
        kernel,
        out_shape=[jax.ShapeDtypeStruct((2, NG * GC, 32, LANES), jnp.float32)] * 2,
        in_specs=[vmem] * 4 + [smem] * 2,
        out_specs=[vmem] * 2,
        scratch_shapes=[
            field(2), face(2, 2), field(), face(2), field(),
            pltpu.VMEM((NG * GC, 32, LANES), jnp.float32),
            field(2), face(2, 2),
            field(), slots, slots, field(), face(2),
            field(2), field(2),
            field(), slots, slots, field(),
            dma((2,)),
            dma((2, NG)), dma((2, NG)),
            dma((2, 1)), dma((2, 1)),
            dma((2, NG)), dma((2, NG)),
            dma((2, NG)), dma((2, NG)),
            dma((4, NG)), dma((4, NG)),
        ],
        compiler_params=pltpu.CompilerParams(
            collective_id=0, has_side_effects=True, vmem_limit_bytes=40 * 1024 * 1024
        ),
    )(rows_of(forcing), rows_of(iterate), rows_of(initial_state), rows_of(damping), mixing, stencil)
    return planes_of(updated), planes_of(defect)


def solution(mesh):
    return jax.shard_map(
        body,
        mesh=mesh,
        in_specs=(
            P("tm", None, "space", None),
            P("tm", None, "space", None),
            P(None, "space", None),
            P(None, "space", None),
            P(),
            P(),
        ),
        out_specs=(P("tm", None, "space", None), P("tm", None, "space", None)),
        check_vma=False,
    )
```

```python
import functools

import jax
import jax.numpy as jnp
from jax import lax
from jax.experimental import pallas as pl
from jax.experimental.pallas import tpu as pltpu
from jax.sharding import PartitionSpec as P

NZ = 64
LANES = 128
wrap_weight = 0.05
MESH = pl.DeviceIdType.MESH
NG, GC = 3, 4


def kernel(
    f_hbm, x_hbm, init_hbm, damp_hbm, mix_ref, st_ref,
    upd_ref, def_ref,
    f_ref, x_ref, init_ref, damp_ref, load_sem,
    part, mine, mine_send, mine_recv, xb, xh, q, qh, ini, prev, a, ah, e, r, co, cc, ch, u, b, e2, r2, co2, c2,
    prev_sem, xh_send, xh_recv, qh_send, qh_recv, ah_send, ah_recv, ch_send, ch_recv,
    s_send, s_recv,
):
    groups = lax.axis_size("tm")
    t = lax.axis_index("tm")
    slabs = lax.axis_size("space")
    s = lax.axis_index("space")
    has_low, has_high = s > 0, s < slabs - 1

    other = lax.rem(s + slabs // 2, slabs)
    z, y = t // 2, t % 2
    partners = [
        lax.rem(z + dz, groups // 2) * 2 + (y + dy) % 2 for dz in (4, 3, 5, 2, 6, 1, 7, 0) for dy in range(2)
    ]

    barrier = pltpu.get_barrier_semaphore()

    def greet(**device):
        pl.semaphore_signal(barrier, inc=1, device_id=device, device_id_type=MESH)

    for partner in partners:
        greet(tm=partner, space=other)
    pl.when(has_low)(lambda: greet(space=s - 1))
    pl.when(has_high)(lambda: greet(space=s + 1))
    pl.when(t > 0)(lambda: greet(tm=t - 1))
    loads = [
        pltpu.make_async_copy(src, dst, load_sem.at[i])
        for i, (src, dst) in enumerate(
            ((x_hbm, x_ref), (damp_hbm, damp_ref), (init_hbm, init_ref), (f_hbm, f_ref))
        )
    ]
    for load in loads:
        load.start()

    lane = lax.broadcasted_iota(jnp.int32, (16, LANES), 1)
    row = lax.broadcasted_iota(jnp.int32, (16, LANES), 0)
    depth = lane % NZ
    half = lane < NZ

    def plane(ref, *index):
        return ref[index].reshape(16, LANES)

    def z_shifts(p):
        before = jnp.where(depth == 0, 0.0, pltpu.roll(p, 1, 1))
        after = jnp.where(depth == NZ - 1, 0.0, pltpu.roll(p, LANES - 1, 1))
        return before, p, after

    def y_before(p):
        turned = pltpu.roll(p, NZ, 1)
        return jnp.where(half, jnp.where(row == 0, 0.0, pltpu.roll(turned, 1, 0)), turned)

    def y_after(p):
        turned = pltpu.roll(p, NZ, 1)
        return jnp.where(half, turned, jnp.where(row == 15, 0.0, pltpu.roll(turned, 15, 0)))

    def taps(sheets, channel):
        shifted = [None if p is None else z_shifts(p) for p in sheets]
        sums = []
        for oy in range(3):
            total = None
            for ox in range(3):
                for oz in range(3):
                    place = ox * 9 + oy * 3 + oz
                    if place == 13 or shifted[ox] is None:
                        continue
                    term = st_ref[channel, place - (place > 13)] * shifted[ox][oz]
                    total = term if total is None else total + term
            sums.append(total)
        return sums[1] + y_before(sums[0]) + y_after(sums[2])

    def to_sides(buf, halo, send, recv, sem):
        def low():
            return pltpu.make_async_remote_copy(
                buf(0), halo(1), send.at[1, sem], recv.at[1, sem], device_id={"space": s - 1}, device_id_type=MESH
            )

        def high():
            return pltpu.make_async_remote_copy(
                buf(1), halo(0), send.at[0, sem], recv.at[0, sem], device_id={"space": s + 1}, device_id_type=MESH
            )

        def start():
            pl.when(has_low)(lambda: low().start())
            pl.when(has_high)(lambda: high().start())

        def wait_recv():
            pl.when(has_low)(lambda: high().wait_recv())
            pl.when(has_high)(lambda: low().wait_recv())

        def wait_send():
            pl.when(has_low)(lambda: low().wait_send())
            pl.when(has_high)(lambda: high().wait_send())

        return start, wait_recv, wait_send

    def x_sides(g):
        return to_sides(lambda x: xb.at[:, g, :, pl.ds(2 * x, 2)], lambda x: xh.at[x, :, g], xh_send, xh_recv, g)

    def q_sides():
        return to_sides(lambda x: q.at[:, :, pl.ds(2 * x, 2)], lambda x: qh.at[x], qh_send, qh_recv, 0)

    def a_sides(g):
        return to_sides(lambda x: a.at[:, g, :, pl.ds(2 * x, 2)], lambda x: ah.at[x, :, g], ah_send, ah_recv, g)

    def c_sides(g):
        return to_sides(lambda x: cc.at[g, :, pl.ds(2 * x, 2)], lambda x: ch.at[x, g], ch_send, ch_recv, g)

    def chunk(ref, g, owner):
        return ref.at[g, owner // 4, owner % 4]

    def gather(src, dst, stage, g):
        for owner in partners:
            pltpu.make_async_remote_copy(
                chunk(src, g, owner), dst.at[g, t], s_send.at[stage, g], s_recv.at[stage, g],
                device_id={"tm": owner, "space": other}, device_id_type=MESH,
            ).start()

    def scatter(src, dst, stage, g):
        for to in partners:
            pltpu.make_async_remote_copy(
                src.at[g, to], chunk(dst, g, t), s_send.at[stage, g], s_recv.at[stage, g],
                device_id={"tm": to, "space": other}, device_id_type=MESH,
            ).start()

    def constants(i):
        src = q if i == 0 else ini
        return pltpu.make_async_remote_copy(
            src.at[:, t // 4, t % 4], mine.at[i], mine_send.at[i], mine_recv.at[i],
            device_id={"space": other}, device_id_type=MESH,
        )

    def await_all(stage, g, sem):
        some = r.at[g]
        pltpu.make_async_copy(some, some, sem.at[stage, g]).wait()

    def solve(src, dst, g, first):
        rate = mine[0, g]
        rate = rate * rate
        total, power = src[g, 0], rate
        for n in range(1, groups):
            total = rate * total + src[g, n]
            power = power * rate
        total = wrap_weight * total if first is None else first + wrap_weight * total
        carry = total / (1.0 - wrap_weight * power)
        for n in range(groups):
            dst[g, n] = carry
            if n < groups - 1:
                carry = rate * carry + src[g, n]

    def split(c, _):
        for n in range(2):
            for x in range(2):
                xb[n, c // GC, c % GC, pl.ds(2 * x, 2)] = x_ref[n, c, pl.ds(x, 16, 2), :].reshape(2, 8, LANES)
        return 0

    def rates(c, _):
        g, i = c // GC, c % GC
        for x in range(2):
            gain = damp_ref[c, pl.ds(x, 16, 2), :] + mix_ref[c, c]
            q[g, i, pl.ds(2 * x, 2)] = (1.0 / (1.0 + gain)).reshape(2, 8, LANES)
            ini[g, i, pl.ds(2 * x, 2)] = init_ref[c, pl.ds(x, 16, 2), :].reshape(2, 8, LANES)
        return 0

    loads[0].wait()
    lax.fori_loop(0, NG * GC, split, 0)
    loads[1].wait()
    loads[2].wait()
    lax.fori_loop(0, NG * GC, rates, 0)
    loads[3].wait()
    edges = has_low.astype(jnp.int32) + has_high.astype(jnp.int32) + (t < groups - 1).astype(jnp.int32)
    pl.semaphore_wait(barrier, groups + edges)

    for g in range(NG):
        x_sides(g)[0]()
    constants(0).start()
    constants(1).start()
    q_sides()[0]()

    def previous():
        return pltpu.make_async_remote_copy(
            x_ref.at[1], prev, prev_sem.at[0], prev_sem.at[1], device_id={"tm": t + 1}, device_id_type=MESH
        )

    pl.when(t < groups - 1)(lambda: previous().start())

    for side, exists in ((0, has_low), (1, has_high)):

        @pl.when(jnp.logical_not(exists))
        def _(side=side):
            xh[side] = jnp.zeros(xh.shape[1:], jnp.float32)
            qh[side] = jnp.zeros(qh.shape[1:], jnp.float32)
            ah[side] = jnp.zeros(ah.shape[1:], jnp.float32)
            ch[side] = jnp.zeros(ch.shape[1:], jnp.float32)

    keep = jnp.where(t < groups - 1, 1.0, 0.0)

    def defects_inside(c, _):
        g, i = c // GC, c % GC
        for n in range(2):
            own = [plane(xb, n, g, i, pl.ds(2 * x, 2)) for x in range(2)]
            for x in range(2):
                near = taps([None, *own] if x == 0 else [*own, None], c)
                applied = damp_ref[c, pl.ds(x, 16, 2), :] * own[x] - near
                for d in range(NG * GC):
                    applied = applied + mix_ref[c, d] * plane(xb, n, d // GC, d % GC, pl.ds(2 * x, 2))
                step = own[x] if n == 0 else own[x] - plane(xb, 0, g, i, pl.ds(2 * x, 2))
                value = f_ref[n, c, pl.ds(x, 16, 2), :] - (step + applied)
                part[n, g, i, pl.ds(2 * x, 2)] = value.reshape(2, 8, LANES)
        return 0

    lax.fori_loop(0, NG * GC, defects_inside, 0)

    def defects(g, _):
        x_sides(g)[1]()

        def channel(i, _):
            c = g * GC + i
            for x in range(2):
                at = pl.ds(2 * x, 2)
                d0, d1 = (
                    plane(part, n, g, i, at)
                    + taps([plane(xh, 0, n, g, i), None, None] if x == 0 else [None, None, plane(xh, 1, n, g, i)], c)
                    for n in range(2)
                )
                rate = plane(q, g, i, at)
                a0 = rate * d0
                a1 = rate * (a0 + d1)
                def_ref[0, c, pl.ds(x, 16, 2), :] = d0
                def_ref[1, c, pl.ds(x, 16, 2), :] = d1
                a[0, g, i, at] = a0.reshape(2, 8, LANES)
                a[1, g, i, at] = a1.reshape(2, 8, LANES)
                e[g, i, at] = (a1 + keep * plane(xb, 1, g, i, at)).reshape(2, 8, LANES)
            return 0

        lax.fori_loop(0, GC, channel, 0)
        gather(e, r, 0, g)
        a_sides(g)[0]()
        return 0

    lax.fori_loop(0, NG, defects, 0)
    constants(0).wait_recv()
    constants(1).wait_recv()

    def carries(g, _):
        await_all(0, g, s_recv)
        solve(r, co, g, mine[1, g])
        scatter(co, cc, 1, g)
        return 0

    lax.fori_loop(0, NG, carries, 0)
    q_sides()[1]()

    def first_sweep(g, _):
        await_all(1, g, s_recv)
        c_sides(g)[0]()

        def channel(i, _):
            rate, carry = q[g, i], cc[g, i]
            moved = rate * carry
            u[0, g, i] = a[0, g, i] + moved
            u[1, g, i] = a[1, g, i] + rate * moved
            for n in range(2):
                own = [plane(u, n, g, i, pl.ds(2 * x, 2)) for x in range(2)]
                for x in range(2):
                    near = taps([None, *own] if x == 0 else [*own, None], g * GC + i)
                    part[n, g, i, pl.ds(2 * x, 2)] = near.reshape(2, 8, LANES)
            return 0

        lax.fori_loop(0, GC, channel, 0)
        return 0

    lax.fori_loop(0, NG, first_sweep, 0)

    def mixed(c, _):
        g, i = c // GC, c % GC
        for n in range(2):
            value = part[n, g, i]
            for d in range(NG * GC):
                value = value - jnp.where(c == d, 0.0, mix_ref[c, d]) * u[n, d // GC, d % GC]
            part[n, g, i] = value
        return 0

    lax.fori_loop(0, NG * GC, mixed, 0)

    def second_sweep(g, _):
        a_sides(g)[1]()
        c_sides(g)[1]()

        def channel(i, _):
            c = g * GC + i
            for x in range(2):
                at = pl.ds(2 * x, 2)
                rate = plane(qh, x, g, i)
                moved = rate * plane(ch, x, g, i)
                halos = (plane(ah, x, 0, g, i) + moved, plane(ah, x, 1, g, i) + rate * moved)
                h0, h1 = (
                    plane(part, n, g, i, at)
                    + taps([halos[n], None, None] if x == 0 else [None, None, halos[n]], c)
                    for n in range(2)
                )
                rate = plane(q, g, i, at)
                v0 = rate * h0
                v1 = rate * (v0 + h1)
                b[0, g, i, at] = (plane(xb, 0, g, i, at) + (plane(u, 0, g, i, at) + v0)).reshape(2, 8, LANES)
                b[1, g, i, at] = (plane(xb, 1, g, i, at) + (plane(u, 1, g, i, at) + v1)).reshape(2, 8, LANES)
                e2[g, i, at] = v1.reshape(2, 8, LANES)
            return 0

        lax.fori_loop(0, GC, channel, 0)
        gather(e2, r2, 2, g)
        return 0

    lax.fori_loop(0, NG, second_sweep, 0)

    def carries_2(g, _):
        await_all(2, g, s_recv)
        solve(r2, co2, g, None)
        scatter(co2, c2, 3, g)
        return 0

    lax.fori_loop(0, NG, carries_2, 0)

    @pl.when(t > 0)
    def _():
        previous().wait_recv()
        def_ref[0] = def_ref[0] + prev[...]

    @pl.when(t == 0)
    def _():
        def_ref[0] = def_ref[0] + init_ref[...]

    def finish(g, _):
        await_all(3, g, s_recv)

        def channel(i, _):
            for x in range(2):
                at = pl.ds(2 * x, 2)
                rate = plane(q, g, i, at)
                moved = rate * plane(c2, g, i, at)
                upd_ref[0, g * GC + i, pl.ds(x, 16, 2), :] = plane(b, 0, g, i, at) + moved
                upd_ref[1, g * GC + i, pl.ds(x, 16, 2), :] = plane(b, 1, g, i, at) + rate * moved
            return 0

        lax.fori_loop(0, GC, channel, 0)
        return 0

    lax.fori_loop(0, NG, finish, 0)

    pl.when(t < groups - 1)(lambda: previous().wait_send())
    q_sides()[2]()
    constants(0).wait_send()
    constants(1).wait_send()
    for g in range(NG):
        x_sides(g)[2]()
        a_sides(g)[2]()
        c_sides(g)[2]()
        for stage in range(4):
            await_all(stage, g, s_send)


def rows_of(value):
    lead = value.shape[:-2]
    value = value.reshape(lead + (2, 16, LANES))
    return jnp.swapaxes(value, -3, -2).reshape(lead + (32, LANES))


def planes_of(value):
    lead = value.shape[:-2]
    value = value.reshape(lead + (16, 2, LANES))
    return jnp.swapaxes(value, -3, -2).reshape(lead + (2, 16 * LANES))


def write(upd_vmem, def_vmem, upd_ref, def_ref, sem):
    copies = [
        pltpu.make_async_copy(upd_vmem, upd_ref, sem.at[0]),
        pltpu.make_async_copy(def_vmem, def_ref, sem.at[1]),
    ]
    for copy in copies:
        copy.start()
    for copy in copies:
        copy.wait()


def body(forcing, iterate, initial_state, damping, mixing, stencil):
    vmem = pl.BlockSpec(memory_space=pltpu.VMEM)
    smem = pl.BlockSpec(memory_space=pltpu.SMEM)
    hbm = pl.BlockSpec(memory_space=pltpu.HBM)

    def field(*lead):
        return pltpu.VMEM((*lead, NG, GC, 4, 8, LANES), jnp.float32)

    def face(*lead):
        return pltpu.VMEM((*lead, NG, GC, 2, 8, LANES), jnp.float32)

    def rows(*lead):
        return pltpu.VMEM((*lead, NG * GC, 32, LANES), jnp.float32)

    slots = pltpu.VMEM((NG, 16, 8, LANES), jnp.float32)
    dma = pltpu.SemaphoreType.DMA
    whole = [jax.ShapeDtypeStruct((2, NG * GC, 32, LANES), jnp.float32)] * 2
    results = pl.pallas_call(
        kernel,
        out_shape=[pltpu.VMEM((2, NG * GC, 32, LANES), jnp.float32)] * 2,
        in_specs=[hbm] * 4 + [smem] * 2,
        out_specs=[vmem] * 2,
        scratch_shapes=[
            rows(2), rows(2), rows(), rows(), dma((4,)),
            field(2), pltpu.VMEM((2, NG, 8, LANES), jnp.float32), dma((2,)), dma((2,)),
            field(2), face(2, 2), field(), face(2), field(),
            rows(),
            field(2), face(2, 2),
            field(), slots, slots, field(), face(2),
            field(2), field(2),
            field(), slots, slots, field(),
            dma((2,)),
            dma((2, NG)), dma((2, NG)),
            dma((2, 1)), dma((2, 1)),
            dma((2, NG)), dma((2, NG)),
            dma((2, NG)), dma((2, NG)),
            dma((4, NG)), dma((4, NG)),
        ],
        compiler_params=pltpu.CompilerParams(
            collective_id=0, has_side_effects=True, vmem_limit_bytes=60 * 1024 * 1024
        ),
    )(rows_of(forcing), rows_of(iterate), rows_of(initial_state), rows_of(damping), mixing, stencil.T)
    updated, defect = pl.pallas_call(
        write, out_shape=whole, in_specs=[vmem] * 2, out_specs=[hbm] * 2, scratch_shapes=[dma((2,))]
    )(*results)
    return planes_of(updated), planes_of(defect)


def solution(mesh):
    return jax.shard_map(
        body,
        mesh=mesh,
        in_specs=(
            P("tm", None, "space", None),
            P("tm", None, "space", None),
            P(None, "space", None),
            P(None, "space", None),
            P(),
            P(),
        ),
        out_specs=(P("tm", None, "space", None), P("tm", None, "space", None)),
        check_vma=False,
    )
```

```python
import functools

import jax
import jax.numpy as jnp
from jax import lax
from jax.experimental import pallas as pl
from jax.experimental.pallas import tpu as pltpu
from jax.sharding import PartitionSpec as P

NZ = 64
LANES = 128
wrap_weight = 0.05
MESH = pl.DeviceIdType.MESH
NG, GC = 3, 4
UNROLL = 4


def kernel(
    f_hbm, x_hbm, init_hbm, damp_hbm, mix_ref, st_ref,
    upd_ref, def_ref,
    f_ref, x_ref, init_ref, damp_ref, load_sem,
    part, aside, mine, mine_send, mine_recv, xb, xh, q, qh, ini, prev, a, ah, e, r, co, cc, ch, u, b, e2, r2, co2, c2,
    prev_send, prev_recv, xh_send, xh_recv, qh_send, qh_recv, ah_send, ah_recv, ch_send, ch_recv,
    s_send, s_recv,
):
    groups = lax.axis_size("tm")
    t = lax.axis_index("tm")
    slabs = lax.axis_size("space")
    s = lax.axis_index("space")
    has_low, has_high = s > 0, s < slabs - 1

    other = lax.rem(s + slabs // 2, slabs)
    z, y = t // 2, t % 2
    partners = [
        lax.rem(z + dz, groups // 2) * 2 + (y + dy) % 2 for dz in (4, 3, 5, 2, 6, 1, 7, 0) for dy in range(2)
    ]

    barrier = pltpu.get_barrier_semaphore()

    def greet(**device):
        pl.semaphore_signal(barrier, inc=1, device_id=device, device_id_type=MESH)

    for partner in partners:
        greet(tm=partner, space=other)
    pl.when(has_low)(lambda: greet(space=s - 1))
    pl.when(has_high)(lambda: greet(space=s + 1))
    pl.when(t > 0)(lambda: greet(tm=t - 1))
    loads = [
        pltpu.make_async_copy(src, dst, load_sem.at[i])
        for i, (src, dst) in enumerate(
            ((x_hbm, x_ref), (damp_hbm, damp_ref), (init_hbm, init_ref), (f_hbm, f_ref))
        )
    ]
    for load in loads:
        load.start()

    lane = lax.broadcasted_iota(jnp.int32, (16, LANES), 1)
    row = lax.broadcasted_iota(jnp.int32, (16, LANES), 0)
    depth = lane % NZ
    half = lane < NZ

    def plane(ref, *index):
        return ref[index].reshape(16, LANES)

    def z_shifts(p):
        before = jnp.where(depth == 0, 0.0, pltpu.roll(p, 1, 1))
        after = jnp.where(depth == NZ - 1, 0.0, pltpu.roll(p, LANES - 1, 1))
        return before, p, after

    def sums_of(sheets, channel):
        sums = []
        for oy in range(3):
            total = None
            for ox in range(3):
                for oz in range(3):
                    place = ox * 9 + oy * 3 + oz
                    if place == 13 or sheets[ox] is None:
                        continue
                    term = st_ref[channel, place - (place > 13)] * sheets[ox][oz]
                    total = term if total is None else total + term
            sums.append(total)
        before, here, after = sums
        above = jnp.where(row == 15, 0.0, pltpu.roll(after, 15, 0))
        below = jnp.where(row == 0, 0.0, pltpu.roll(before, 1, 0))
        return here, jnp.where(half, before + above, below + after)

    def turn(p):
        return pltpu.roll(p, NZ, 1)

    def tile(p):
        return p.reshape(2, 8, LANES)

    def to_sides(buf, halo, send, recv, sem):
        def low():
            return pltpu.make_async_remote_copy(
                buf(0), halo(1), send.at[1, sem], recv.at[1, sem], device_id={"space": s - 1}, device_id_type=MESH
            )

        def high():
            return pltpu.make_async_remote_copy(
                buf(1), halo(0), send.at[0, sem], recv.at[0, sem], device_id={"space": s + 1}, device_id_type=MESH
            )

        def start():
            pl.when(has_low)(lambda: low().start())
            pl.when(has_high)(lambda: high().start())

        def wait_recv():
            pl.when(has_low)(lambda: high().wait_recv())
            pl.when(has_high)(lambda: low().wait_recv())

        def wait_send():
            pl.when(has_low)(lambda: low().wait_send())
            pl.when(has_high)(lambda: high().wait_send())

        return start, wait_recv, wait_send

    def x_sides(g):
        return to_sides(lambda x: xb.at[:, g, :, pl.ds(2 * x, 2)], lambda x: xh.at[x, :, g], xh_send, xh_recv, g)

    def q_sides():
        return to_sides(lambda x: q.at[:, :, pl.ds(2 * x, 2)], lambda x: qh.at[x], qh_send, qh_recv, 0)

    def a_sides(g):
        return to_sides(lambda x: a.at[:, g, :, pl.ds(2 * x, 2)], lambda x: ah.at[x, :, g], ah_send, ah_recv, g)

    def c_sides(g):
        return to_sides(lambda x: cc.at[g, :, pl.ds(2 * x, 2)], lambda x: ch.at[x, g], ch_send, ch_recv, g)

    def chunk(ref, g, owner):
        return ref.at[g, owner // 4, owner % 4]

    def gather(src, dst, stage, g):
        for owner in partners:
            pltpu.make_async_remote_copy(
                chunk(src, g, owner), dst.at[g, t], s_send.at[stage, g], s_recv.at[stage, g],
                device_id={"tm": owner, "space": other}, device_id_type=MESH,
            ).start()

    def scatter(src, dst, stage, g):
        for to in partners:
            pltpu.make_async_remote_copy(
                src.at[g, to], chunk(dst, g, t), s_send.at[stage, g], s_recv.at[stage, g],
                device_id={"tm": to, "space": other}, device_id_type=MESH,
            ).start()

    def constants(i):
        src = q if i == 0 else ini
        return pltpu.make_async_remote_copy(
            src.at[:, t // 4, t % 4], mine.at[i], mine_send.at[i], mine_recv.at[i],
            device_id={"space": other}, device_id_type=MESH,
        )

    def await_all(stage, g, sem):
        some = r.at[g]
        pltpu.make_async_copy(some, some, sem.at[stage, g]).wait()

    def solve(src, dst, g, first):
        rate = mine[0, g]
        rate = rate * rate
        total, power = src[g, 0], rate
        for n in range(1, groups):
            total = rate * total + src[g, n]
            power = power * rate
        total = wrap_weight * total if first is None else first + wrap_weight * total
        carry = total / (1.0 - wrap_weight * power)
        for n in range(groups):
            dst[g, n] = carry
            if n < groups - 1:
                carry = rate * carry + src[g, n]

    def split(c, _):
        for n in range(2):
            for x in range(2):
                xb[n, c // GC, c % GC, pl.ds(2 * x, 2)] = x_ref[n, c, pl.ds(x, 16, 2), :].reshape(2, 8, LANES)
        return 0

    def rates(c, _):
        g, i = c // GC, c % GC
        for x in range(2):
            gain = damp_ref[c, pl.ds(x, 16, 2), :] + mix_ref[c, c]
            q[g, i, pl.ds(2 * x, 2)] = (1.0 / (1.0 + gain)).reshape(2, 8, LANES)
            ini[g, i, pl.ds(2 * x, 2)] = init_ref[c, pl.ds(x, 16, 2), :].reshape(2, 8, LANES)
        return 0

    loads[0].wait()
    lax.fori_loop(0, NG * GC, split, 0)
    loads[1].wait()
    loads[2].wait()
    lax.fori_loop(0, NG * GC, rates, 0)
    loads[3].wait()
    edges = has_low.astype(jnp.int32) + has_high.astype(jnp.int32) + (t < groups - 1).astype(jnp.int32)
    pl.semaphore_wait(barrier, groups + edges)

    for g in range(NG):
        x_sides(g)[0]()
    constants(0).start()
    constants(1).start()

    def previous(h):
        some = pl.ds(6 * h, 6)
        return pltpu.make_async_remote_copy(
            x_ref.at[1, some], prev.at[some], prev_send.at[h], prev_recv.at[h],
            device_id={"tm": t + 1}, device_id_type=MESH,
        )

    pl.when(t < groups - 1)(lambda: previous(0).start())

    for side, exists in ((0, has_low), (1, has_high)):

        @pl.when(jnp.logical_not(exists))
        def _(side=side):
            xh[side] = jnp.zeros(xh.shape[1:], jnp.float32)
            qh[side] = jnp.zeros(qh.shape[1:], jnp.float32)
            ah[side] = jnp.zeros(ah.shape[1:], jnp.float32)
            ch[side] = jnp.zeros(ch.shape[1:], jnp.float32)

    keep = jnp.where(t < groups - 1, 1.0, 0.0)

    def defects_inside(c, _):
        g, i = c // GC, c % GC
        for n in range(2):
            own = [plane(xb, n, g, i, pl.ds(2 * x, 2)) for x in range(2)]
            moved = [z_shifts(p) for p in own]
            for x in range(2):
                at = pl.ds(2 * x, 2)
                here, turned = sums_of([None, *moved] if x == 0 else [*moved, None], c)
                value = f_ref[n, c, pl.ds(x, 16, 2), :] - own[x] - damp_ref[c, pl.ds(x, 16, 2), :] * own[x] + here
                for d in range(NG * GC):
                    value = value - mix_ref[c, d] * plane(xb, n, d // GC, d % GC, at)
                if n == 1:
                    value = value + plane(xb, 0, g, i, at)
                part[n, g, i, at] = tile(value)
                aside[n, g, i, at] = tile(turned)
        return 0

    lax.fori_loop(0, NG * GC, defects_inside, 0, unroll=UNROLL)

    def defects(g, _):
        x_sides(g)[1]()

        def channel(i, _):
            c = g * GC + i
            for x in range(2):
                at = pl.ds(2 * x, 2)
                values = []
                for n in range(2):
                    moved = z_shifts(plane(xh, x, n, g, i))
                    here, turned = sums_of([moved, None, None] if x == 0 else [None, None, moved], c)
                    values.append(plane(part, n, g, i, at) + here + turn(plane(aside, n, g, i, at) + turned))
                d0, d1 = values
                rate = plane(q, g, i, at)
                a0 = rate * d0
                a1 = rate * (a0 + d1)
                def_ref[0, c, pl.ds(x, 16, 2), :] = d0
                def_ref[1, c, pl.ds(x, 16, 2), :] = d1
                a[0, g, i, at] = tile(a0)
                a[1, g, i, at] = tile(a1)
                e[g, i, at] = tile(a1 + keep * plane(xb, 1, g, i, at))
            return 0

        lax.fori_loop(0, GC, channel, 0, unroll=UNROLL)
        gather(e, r, 0, g)
        return 0

    lax.fori_loop(0, NG, defects, 0)
    for g in range(NG):
        a_sides(g)[0]()
    q_sides()[0]()
    constants(0).wait_recv()
    constants(1).wait_recv()

    def carries(g, _):
        await_all(0, g, s_recv)
        solve(r, co, g, mine[1, g])
        scatter(co, cc, 1, g)
        return 0

    lax.fori_loop(0, NG, carries, 0)

    def first_sweep(g, _):
        await_all(1, g, s_recv)
        c_sides(g)[0]()

        def channel(i, _):
            rate, carry = q[g, i], cc[g, i]
            moved = rate * carry
            u[0, g, i] = a[0, g, i] + moved
            u[1, g, i] = a[1, g, i] + rate * moved
            for n in range(2):
                moved = [z_shifts(plane(u, n, g, i, pl.ds(2 * x, 2))) for x in range(2)]
                for x in range(2):
                    at = pl.ds(2 * x, 2)
                    here, turned = sums_of([None, *moved] if x == 0 else [*moved, None], g * GC + i)
                    part[n, g, i, at] = tile(here)
                    aside[n, g, i, at] = tile(turned)
            return 0

        lax.fori_loop(0, GC, channel, 0, unroll=UNROLL)
        return 0

    lax.fori_loop(0, NG, first_sweep, 0)
    pl.when(t < groups - 1)(lambda: previous(1).start())

    def mixed(c, _):
        g, i = c // GC, c % GC
        for n in range(2):
            value = part[n, g, i]
            for d in range(NG * GC):
                value = value - jnp.where(c == d, 0.0, mix_ref[c, d]) * u[n, d // GC, d % GC]
            part[n, g, i] = value
        return 0

    lax.fori_loop(0, NG * GC, mixed, 0, unroll=UNROLL)
    q_sides()[1]()

    def second_sweep(g, _):
        a_sides(g)[1]()
        c_sides(g)[1]()

        def channel(i, _):
            c = g * GC + i
            for x in range(2):
                at = pl.ds(2 * x, 2)
                rate = plane(qh, x, g, i)
                moved = rate * plane(ch, x, g, i)
                halos = (plane(ah, x, 0, g, i) + moved, plane(ah, x, 1, g, i) + rate * moved)
                values = []
                for n in range(2):
                    moved = z_shifts(halos[n])
                    here, turned = sums_of([moved, None, None] if x == 0 else [None, None, moved], c)
                    values.append(plane(part, n, g, i, at) + here + turn(plane(aside, n, g, i, at) + turned))
                h0, h1 = values
                rate = plane(q, g, i, at)
                v0 = rate * h0
                v1 = rate * (v0 + h1)
                e2[g, i, at] = tile(v1)
                b[0, g, i, at] = tile(plane(xb, 0, g, i, at) + (plane(u, 0, g, i, at) + v0))
                b[1, g, i, at] = tile(plane(xb, 1, g, i, at) + (plane(u, 1, g, i, at) + v1))
            return 0

        lax.fori_loop(0, GC, channel, 0, unroll=UNROLL)
        gather(e2, r2, 2, g)
        return 0

    lax.fori_loop(0, NG, second_sweep, 0)

    def carries_2(g, _):
        await_all(2, g, s_recv)
        solve(r2, co2, g, None)
        scatter(co2, c2, 3, g)
        return 0

    lax.fori_loop(0, NG, carries_2, 0)

    @pl.when(t > 0)
    def _():
        previous(0).wait_recv()
        previous(1).wait_recv()
        def_ref[0] = def_ref[0] + prev[...]

    @pl.when(t == 0)
    def _():
        def_ref[0] = def_ref[0] + init_ref[...]

    def finish(g, _):
        await_all(3, g, s_recv)

        def channel(i, _):
            for x in range(2):
                at = pl.ds(2 * x, 2)
                rate = plane(q, g, i, at)
                moved = rate * plane(c2, g, i, at)
                upd_ref[0, g * GC + i, pl.ds(x, 16, 2), :] = plane(b, 0, g, i, at) + moved
                upd_ref[1, g * GC + i, pl.ds(x, 16, 2), :] = plane(b, 1, g, i, at) + rate * moved
            return 0

        lax.fori_loop(0, GC, channel, 0)
        return 0

    lax.fori_loop(0, NG, finish, 0)

    pl.when(t < groups - 1)(lambda: previous(0).wait_send())
    pl.when(t < groups - 1)(lambda: previous(1).wait_send())
    q_sides()[2]()
    constants(0).wait_send()
    constants(1).wait_send()
    for g in range(NG):
        x_sides(g)[2]()
        a_sides(g)[2]()
        c_sides(g)[2]()
        for stage in range(4):
            await_all(stage, g, s_send)


def rows_of(value):
    lead = value.shape[:-2]
    value = value.reshape(lead + (2, 16, LANES))
    return jnp.swapaxes(value, -3, -2).reshape(lead + (32, LANES))


def planes_of(value):
    lead = value.shape[:-2]
    value = value.reshape(lead + (16, 2, LANES))
    return jnp.swapaxes(value, -3, -2).reshape(lead + (2, 16 * LANES))


def body(forcing, iterate, initial_state, damping, mixing, stencil):
    vmem = pl.BlockSpec(memory_space=pltpu.VMEM)
    smem = pl.BlockSpec(memory_space=pltpu.SMEM)
    hbm = pl.BlockSpec(memory_space=pltpu.HBM)

    def field(*lead):
        return pltpu.VMEM((*lead, NG, GC, 4, 8, LANES), jnp.float32)

    def face(*lead):
        return pltpu.VMEM((*lead, NG, GC, 2, 8, LANES), jnp.float32)

    def rows(*lead):
        return pltpu.VMEM((*lead, NG * GC, 32, LANES), jnp.float32)

    slots = pltpu.VMEM((NG, 16, 8, LANES), jnp.float32)
    dma = pltpu.SemaphoreType.DMA
    updated, defect = pl.pallas_call(
        kernel,
        out_shape=[rows(2)] * 2,
        in_specs=[hbm] * 4 + [smem] * 2,
        out_specs=[vmem] * 2,
        scratch_shapes=[
            rows(2), rows(2), rows(), rows(), dma((4,)),
            field(2), field(2), pltpu.VMEM((2, NG, 8, LANES), jnp.float32), dma((2,)), dma((2,)),
            field(2), face(2, 2), field(), face(2), field(),
            rows(),
            field(2), face(2, 2),
            field(), slots, slots, field(), face(2),
            field(2), field(2),
            field(), slots, slots, field(),
            dma((2,)), dma((2,)),
            dma((2, NG)), dma((2, NG)),
            dma((2, 1)), dma((2, 1)),
            dma((2, NG)), dma((2, NG)),
            dma((2, NG)), dma((2, NG)),
            dma((4, NG)), dma((4, NG)),
        ],
        compiler_params=pltpu.CompilerParams(
            collective_id=0, has_side_effects=True, vmem_limit_bytes=60 * 1024 * 1024
        ),
    )(rows_of(forcing), rows_of(iterate), rows_of(initial_state), rows_of(damping), mixing, stencil.T)
    return planes_of(updated), planes_of(defect)


def solution(mesh):
    return jax.shard_map(
        body,
        mesh=mesh,
        in_specs=(
            P("tm", None, "space", None),
            P("tm", None, "space", None),
            P(None, "space", None),
            P(None, "space", None),
            P(),
            P(),
        ),
        out_specs=(P("tm", None, "space", None), P("tm", None, "space", None)),
        check_vma=False,
    )
```

```python
import functools

import jax
import jax.numpy as jnp
from jax import lax
from jax.experimental import pallas as pl
from jax.experimental.pallas import tpu as pltpu
from jax.sharding import PartitionSpec as P

NZ = 64
LANES = 128
wrap_weight = 0.05
MESH = pl.DeviceIdType.MESH
NG, GC = 3, 4
UNROLL = 4
CUT = 6


def kernel(
    f_hbm, x_hbm, init_hbm, damp_hbm, mix_hbm, st_hbm,
    out_ref,
    f_ref, x_ref, init_ref, damp_ref, mix_ref, st_ref, load_sem, second, third,
    part, aside, mine, mine_send, mine_recv, xb, xh, q, qh, ini, prev, a, ah, e, r, co, cc, ch, u, b, e2, r2, co2, c2,
    prev_send, prev_recv, xh_send, xh_recv, qh_send, qh_recv, ah_send, ah_recv, ch_send, ch_recv,
    s_send, s_recv,
):
    upd_ref, def_ref = out_ref.at[0], out_ref.at[1]
    groups = lax.axis_size("tm")
    t = lax.axis_index("tm")
    slabs = lax.axis_size("space")
    s = lax.axis_index("space")
    has_low, has_high = s > 0, s < slabs - 1

    other = lax.rem(s + slabs // 2, slabs)
    z, y = t // 2, t % 2
    partners = [
        lax.rem(z + dz, groups // 2) * 2 + (y + dy) % 2 for dz in (4, 3, 5, 2, 6, 1, 7, 0) for dy in range(2)
    ]

    barrier = pltpu.get_barrier_semaphore()
    around = [{"tm": lax.rem(z + dz, groups // 2) * 2 + y} for dz in (2, groups // 2 - 2, 1, groups // 2 - 1)]
    flip = [{"tm": 2 * z + 1 - y}]
    across = [{"tm": 2 * z + dy, "space": other} for dy in range(2)]

    def greet(sem, devices):
        for device in devices:
            pl.semaphore_signal(sem, inc=1, device_id=device, device_id_type=MESH)

    greet(barrier, around + across + flip)
    pl.when(has_low)(lambda: greet(barrier, [{"space": s - 1}]))
    pl.when(has_high)(lambda: greet(barrier, [{"space": s + 1}]))
    loads = [
        pltpu.make_async_copy(src, dst, load_sem.at[i])
        for i, (src, dst) in enumerate(
            ((x_hbm, x_ref), (mix_hbm, mix_ref), (st_hbm, st_ref), (damp_hbm, damp_ref), (init_hbm, init_ref), (f_hbm, f_ref))
        )
    ]
    for load in loads:
        load.start()

    lane = lax.broadcasted_iota(jnp.int32, (16, LANES), 1)
    row = lax.broadcasted_iota(jnp.int32, (16, LANES), 0)
    depth = lane % NZ
    half = lane < NZ

    def plane(ref, *index):
        return ref[index].reshape(16, LANES)

    def z_shifts(p):
        before = jnp.where(depth == 0, 0.0, pltpu.roll(p, 1, 1))
        after = jnp.where(depth == NZ - 1, 0.0, pltpu.roll(p, LANES - 1, 1))
        return before, p, after

    def sums_of(sheets, channel):
        sums = []
        for oy in range(3):
            total = None
            for ox in range(3):
                for oz in range(3):
                    place = ox * 9 + oy * 3 + oz
                    if place == 13 or sheets[ox] is None:
                        continue
                    term = st_ref[channel, place - (place > 13)] * sheets[ox][oz]
                    total = term if total is None else total + term
            sums.append(total)
        before, here, after = sums
        above = jnp.where(row == 15, 0.0, pltpu.roll(after, 15, 0))
        below = jnp.where(row == 0, 0.0, pltpu.roll(before, 1, 0))
        return here, jnp.where(half, before + above, below + after)

    def turn(p):
        return pltpu.roll(p, NZ, 1)

    def tile(p):
        return p.reshape(2, 8, LANES)

    def to_sides(buf, halo, send, recv, sem):
        def low():
            return pltpu.make_async_remote_copy(
                buf(0), halo(1), send.at[1, sem], recv.at[1, sem], device_id={"space": s - 1}, device_id_type=MESH
            )

        def high():
            return pltpu.make_async_remote_copy(
                buf(1), halo(0), send.at[0, sem], recv.at[0, sem], device_id={"space": s + 1}, device_id_type=MESH
            )

        def start():
            pl.when(has_low)(lambda: low().start())
            pl.when(has_high)(lambda: high().start())

        def wait_recv():
            pl.when(has_low)(lambda: high().wait_recv())
            pl.when(has_high)(lambda: low().wait_recv())

        def wait_send():
            pl.when(has_low)(lambda: low().wait_send())
            pl.when(has_high)(lambda: high().wait_send())

        return start, wait_recv, wait_send

    def x_sides(g):
        return to_sides(lambda x: xb.at[:, g, :, pl.ds(2 * x, 2)], lambda x: xh.at[x, :, g], xh_send, xh_recv, g)

    def q_sides():
        return to_sides(lambda x: q.at[:, :, pl.ds(2 * x, 2)], lambda x: qh.at[x], qh_send, qh_recv, 0)

    def a_sides(g):
        return to_sides(lambda x: a.at[:, g, :, pl.ds(2 * x, 2)], lambda x: ah.at[x, :, g], ah_send, ah_recv, g)

    def c_sides(g):
        return to_sides(lambda x: cc.at[g, :, pl.ds(2 * x, 2)], lambda x: ch.at[x, g], ch_send, ch_recv, g)

    def chunk(ref, g, owner):
        return ref.at[g, owner // 4, owner % 4]

    def gather(src, dst, stage, g):
        for owner in partners:
            pltpu.make_async_remote_copy(
                chunk(src, g, owner), dst.at[g, t], s_send.at[stage, g], s_recv.at[stage, g],
                device_id={"tm": owner, "space": other}, device_id_type=MESH,
            ).start()

    def scatter(src, dst, stage, g):
        for to in partners:
            pltpu.make_async_remote_copy(
                src.at[g, to], chunk(dst, g, t), s_send.at[stage, g], s_recv.at[stage, g],
                device_id={"tm": to, "space": other}, device_id_type=MESH,
            ).start()

    def constants(i):
        src = q if i == 0 else ini
        return pltpu.make_async_remote_copy(
            src.at[:, t // 4, t % 4], mine.at[i], mine_send.at[i], mine_recv.at[i],
            device_id={"space": other}, device_id_type=MESH,
        )

    def await_all(stage, g, sem):
        some = r.at[g]
        pltpu.make_async_copy(some, some, sem.at[stage, g]).wait()

    def solve(src, dst, g, first):
        rate = mine[0, g]
        rate = rate * rate
        total, power = src[g, 0], rate
        for n in range(1, groups):
            total = rate * total + src[g, n]
            power = power * rate
        total = wrap_weight * total if first is None else first + wrap_weight * total
        carry = total / (1.0 - wrap_weight * power)
        for n in range(groups):
            dst[g, n] = carry
            if n < groups - 1:
                carry = rate * carry + src[g, n]

    def split(c, _):
        for n in range(2):
            for x in range(2):
                xb[n, c // GC, c % GC, pl.ds(2 * x, 2)] = x_ref[n, c, pl.ds(x, 16, 2), :].reshape(2, 8, LANES)
        return 0

    def rates(c, _):
        g, i = c // GC, c % GC
        for x in range(2):
            gain = damp_ref[c, pl.ds(x, 16, 2), :] + mix_ref[c, c]
            q[g, i, pl.ds(2 * x, 2)] = (1.0 / (1.0 + gain)).reshape(2, 8, LANES)
            ini[g, i, pl.ds(2 * x, 2)] = init_ref[c, pl.ds(x, 16, 2), :].reshape(2, 8, LANES)
        return 0

    loads[0].wait()
    lax.fori_loop(0, NG * GC, split, 0)
    for load in loads[1:5]:
        load.wait()
    lax.fori_loop(0, NG * GC, rates, 0)
    loads[5].wait()
    edges = has_low.astype(jnp.int32) + has_high.astype(jnp.int32)
    pl.semaphore_wait(barrier, len(around + across + flip) + edges)
    greet(second, around + across)

    for g in range(NG):
        x_sides(g)[0]()
    constants(0).start()
    constants(1).start()

    def previous(h):
        some = pl.ds(CUT * h, CUT + h * (NG * GC - 2 * CUT))
        return pltpu.make_async_remote_copy(
            x_ref.at[1, some], prev.at[some], prev_send.at[h], prev_recv.at[h],
            device_id={"tm": t + 1}, device_id_type=MESH,
        )

    for side, exists in ((0, has_low), (1, has_high)):

        @pl.when(jnp.logical_not(exists))
        def _(side=side):
            xh[side] = jnp.zeros(xh.shape[1:], jnp.float32)
            qh[side] = jnp.zeros(qh.shape[1:], jnp.float32)
            ah[side] = jnp.zeros(ah.shape[1:], jnp.float32)
            ch[side] = jnp.zeros(ch.shape[1:], jnp.float32)

    keep = jnp.where(t < groups - 1, 1.0, 0.0)

    def defects_inside(c, _):
        g, i = c // GC, c % GC
        for n in range(2):
            own = [plane(xb, n, g, i, pl.ds(2 * x, 2)) for x in range(2)]
            moved = [z_shifts(p) for p in own]
            for x in range(2):
                at = pl.ds(2 * x, 2)
                here, turned = sums_of([None, *moved] if x == 0 else [*moved, None], c)
                value = f_ref[n, c, pl.ds(x, 16, 2), :] - own[x] - damp_ref[c, pl.ds(x, 16, 2), :] * own[x] + here
                for d in range(NG * GC):
                    value = value - mix_ref[c, d] * plane(xb, n, d // GC, d % GC, at)
                if n == 1:
                    value = value + plane(xb, 0, g, i, at)
                part[n, g, i, at] = tile(value)
                aside[n, g, i, at] = tile(turned)
        return 0

    pl.semaphore_wait(second, len(around + across))
    greet(third, around)
    pl.when(t < groups - 1)(lambda: previous(0).start())
    lax.fori_loop(0, NG * GC, defects_inside, 0, unroll=UNROLL)

    def defects(g, _):
        x_sides(g)[1]()

        def channel(i, _):
            c = g * GC + i
            for x in range(2):
                at = pl.ds(2 * x, 2)
                values = []
                for n in range(2):
                    moved = z_shifts(plane(xh, x, n, g, i))
                    here, turned = sums_of([moved, None, None] if x == 0 else [None, None, moved], c)
                    values.append(plane(part, n, g, i, at) + here + turn(plane(aside, n, g, i, at) + turned))
                d0, d1 = values
                rate = plane(q, g, i, at)
                a0 = rate * d0
                a1 = rate * (a0 + d1)
                def_ref[0, c, pl.ds(x, 16, 2), :] = d0
                def_ref[1, c, pl.ds(x, 16, 2), :] = d1
                a[0, g, i, at] = tile(a0)
                a[1, g, i, at] = tile(a1)
                e[g, i, at] = tile(a1 + keep * plane(xb, 1, g, i, at))
            return 0

        lax.fori_loop(0, GC, channel, 0, unroll=UNROLL)
        pl.when(g == 0)(lambda: pl.semaphore_wait(third, len(around)))
        gather(e, r, 0, g)
        return 0

    lax.fori_loop(0, NG, defects, 0)
    for g in range(NG):
        a_sides(g)[0]()
    q_sides()[0]()
    constants(0).wait_recv()
    constants(1).wait_recv()

    def carries(g, _):
        await_all(0, g, s_recv)
        solve(r, co, g, mine[1, g])
        scatter(co, cc, 1, g)
        return 0

    lax.fori_loop(0, NG, carries, 0)

    def first_sweep(g, _):
        await_all(1, g, s_recv)
        c_sides(g)[0]()

        def channel(i, _):
            rate, carry = q[g, i], cc[g, i]
            moved = rate * carry
            u[0, g, i] = a[0, g, i] + moved
            u[1, g, i] = a[1, g, i] + rate * moved
            for n in range(2):
                moved = [z_shifts(plane(u, n, g, i, pl.ds(2 * x, 2))) for x in range(2)]
                for x in range(2):
                    at = pl.ds(2 * x, 2)
                    here, turned = sums_of([None, *moved] if x == 0 else [*moved, None], g * GC + i)
                    part[n, g, i, at] = tile(here)
                    aside[n, g, i, at] = tile(turned)
            return 0

        lax.fori_loop(0, GC, channel, 0, unroll=UNROLL)
        return 0

    lax.fori_loop(0, NG, first_sweep, 0)
    pl.when(t < groups - 1)(lambda: previous(1).start())

    def mixed(c, _):
        g, i = c // GC, c % GC
        for n in range(2):
            value = part[n, g, i]
            for d in range(NG * GC):
                value = value - jnp.where(c == d, 0.0, mix_ref[c, d]) * u[n, d // GC, d % GC]
            part[n, g, i] = value
        return 0

    lax.fori_loop(0, NG * GC, mixed, 0, unroll=UNROLL)
    q_sides()[1]()

    def second_sweep(g, _):
        a_sides(g)[1]()
        c_sides(g)[1]()

        def channel(i, _):
            c = g * GC + i
            for x in range(2):
                at = pl.ds(2 * x, 2)
                rate = plane(qh, x, g, i)
                moved = rate * plane(ch, x, g, i)
                halos = (plane(ah, x, 0, g, i) + moved, plane(ah, x, 1, g, i) + rate * moved)
                values = []
                for n in range(2):
                    moved = z_shifts(halos[n])
                    here, turned = sums_of([moved, None, None] if x == 0 else [None, None, moved], c)
                    values.append(plane(part, n, g, i, at) + here + turn(plane(aside, n, g, i, at) + turned))
                h0, h1 = values
                rate = plane(q, g, i, at)
                v0 = rate * h0
                v1 = rate * (v0 + h1)
                e2[g, i, at] = tile(v1)
                b[0, g, i, at] = tile(plane(xb, 0, g, i, at) + (plane(u, 0, g, i, at) + v0))
                b[1, g, i, at] = tile(plane(xb, 1, g, i, at) + (plane(u, 1, g, i, at) + v1))
            return 0

        lax.fori_loop(0, GC, channel, 0, unroll=UNROLL)
        gather(e2, r2, 2, g)
        return 0

    lax.fori_loop(0, NG, second_sweep, 0)

    def carries_2(g, _):
        await_all(2, g, s_recv)
        solve(r2, co2, g, None)
        scatter(co2, c2, 3, g)
        return 0

    lax.fori_loop(0, NG, carries_2, 0)

    @pl.when(t > 0)
    def _():
        previous(0).wait_recv()
        previous(1).wait_recv()
        def_ref[0] = def_ref[0] + prev[...]

    @pl.when(t == 0)
    def _():
        def_ref[0] = def_ref[0] + init_ref[...]

    def finish(g, _):
        await_all(3, g, s_recv)

        def channel(i, _):
            for x in range(2):
                at = pl.ds(2 * x, 2)
                rate = plane(q, g, i, at)
                moved = rate * plane(c2, g, i, at)
                upd_ref[0, g * GC + i, pl.ds(x, 16, 2), :] = plane(b, 0, g, i, at) + moved
                upd_ref[1, g * GC + i, pl.ds(x, 16, 2), :] = plane(b, 1, g, i, at) + rate * moved
            return 0

        lax.fori_loop(0, GC, channel, 0)
        return 0

    lax.fori_loop(0, NG, finish, 0)

    pl.when(t < groups - 1)(lambda: previous(0).wait_send())
    pl.when(t < groups - 1)(lambda: previous(1).wait_send())
    q_sides()[2]()
    constants(0).wait_send()
    constants(1).wait_send()
    for g in range(NG):
        x_sides(g)[2]()
        a_sides(g)[2]()
        c_sides(g)[2]()
        for stage in range(4):
            await_all(stage, g, s_send)


def rows_of(value):
    lead = value.shape[:-2]
    value = value.reshape(lead + (2, 16, LANES))
    return jnp.swapaxes(value, -3, -2).reshape(lead + (32, LANES))


def planes_of(value):
    lead = value.shape[:-2]
    value = value.reshape(lead + (16, 2, LANES))
    return jnp.swapaxes(value, -3, -2).reshape(lead + (2, 16 * LANES))


def body(forcing, iterate, initial_state, damping, mixing, stencil):
    vmem = pl.BlockSpec(memory_space=pltpu.VMEM)
    hbm = pl.BlockSpec(memory_space=pltpu.HBM)

    def field(*lead):
        return pltpu.VMEM((*lead, NG, GC, 4, 8, LANES), jnp.float32)

    def face(*lead):
        return pltpu.VMEM((*lead, NG, GC, 2, 8, LANES), jnp.float32)

    def rows(*lead):
        return pltpu.VMEM((*lead, NG * GC, 32, LANES), jnp.float32)

    slots = pltpu.VMEM((NG, 16, 8, LANES), jnp.float32)
    dma = pltpu.SemaphoreType.DMA
    results = pl.pallas_call(
        kernel,
        out_shape=rows(2, 2),
        in_specs=[hbm] * 6,
        out_specs=vmem,
        scratch_shapes=[
            rows(2), rows(2), rows(), rows(),
            pltpu.SMEM((NG * GC, NG * GC), jnp.float32), pltpu.SMEM((NG * GC, 26), jnp.float32), dma((6,)),
            pltpu.SemaphoreType.REGULAR, pltpu.SemaphoreType.REGULAR,
            field(2), field(2), pltpu.VMEM((2, NG, 8, LANES), jnp.float32), dma((2,)), dma((2,)),
            field(2), face(2, 2), field(), face(2), field(),
            rows(),
            field(2), face(2, 2),
            field(), slots, slots, field(), face(2),
            field(2), field(2),
            field(), slots, slots, field(),
            dma((2,)), dma((2,)),
            dma((2, NG)), dma((2, NG)),
            dma((2, 1)), dma((2, 1)),
            dma((2, NG)), dma((2, NG)),
            dma((2, NG)), dma((2, NG)),
            dma((4, NG)), dma((4, NG)),
        ],
        compiler_params=pltpu.CompilerParams(
            collective_id=0, has_side_effects=True, vmem_limit_bytes=60 * 1024 * 1024
        ),
    )(rows_of(forcing), rows_of(iterate), rows_of(initial_state), rows_of(damping), mixing, stencil.T)
    return planes_of(results[0]), planes_of(results[1])


def solution(mesh):
    return jax.shard_map(
        body,
        mesh=mesh,
        in_specs=(
            P("tm", None, "space", None),
            P("tm", None, "space", None),
            P(None, "space", None),
            P(None, "space", None),
            P(),
            P(),
        ),
        out_specs=(P("tm", None, "space", None), P("tm", None, "space", None)),
        check_vma=False,
    )
```

```python
import functools

import jax
import jax.numpy as jnp
from jax import lax
from jax.experimental import pallas as pl
from jax.experimental.pallas import tpu as pltpu
from jax.sharding import PartitionSpec as P

NZ = 64
LANES = 128
wrap_weight = 0.05
MESH = pl.DeviceIdType.MESH
NG, GC = 3, 4
UNROLL = 4
CUT = 6


def kernel(
    f_hbm, x_hbm, init_hbm, damp_hbm, mix_hbm, st_hbm,
    out_ref,
    f_ref, x_ref, init_ref, damp_ref, mix_ref, st_ref, load_sem, second, third,
    part, aside, mine, mine_send, mine_recv, xb, xh, q, qh, ini, prev, a, ah, e, r, co, cc, ch, u, b, e2, r2, co2, c2,
    prev_send, prev_recv, xh_send, xh_recv, qh_send, qh_recv, ah_send, ah_recv, ch_send, ch_recv,
    s_send, s_recv,
):
    upd_ref, def_ref = out_ref.at[0], out_ref.at[1]
    groups = lax.axis_size("tm")
    t = lax.axis_index("tm")
    slabs = lax.axis_size("space")
    s = lax.axis_index("space")
    has_low, has_high = s > 0, s < slabs - 1

    other = lax.rem(s + slabs // 2, slabs)
    z, y = t // 2, t % 2
    partners = [
        lax.rem(z + dz, groups // 2) * 2 + (y + dy) % 2 for dz in (4, 3, 5, 2, 6, 1, 7, 0) for dy in range(2)
    ]

    barrier = pltpu.get_barrier_semaphore()
    around = [{"tm": lax.rem(z + dz, groups // 2) * 2 + y} for dz in (2, groups // 2 - 2, 1, groups // 2 - 1)]
    flip = [{"tm": 2 * z + 1 - y}]
    across = [{"tm": 2 * z + dy, "space": other} for dy in range(2)]

    def greet(sem, devices):
        for device in devices:
            pl.semaphore_signal(sem, inc=1, device_id=device, device_id_type=MESH)

    greet(barrier, around + across + flip)
    pl.when(has_low)(lambda: greet(barrier, [{"space": s - 1}]))
    pl.when(has_high)(lambda: greet(barrier, [{"space": s + 1}]))
    loads = [
        pltpu.make_async_copy(src, dst, load_sem.at[i])
        for i, (src, dst) in enumerate(
            ((x_hbm, x_ref), (mix_hbm, mix_ref), (st_hbm, st_ref), (damp_hbm, damp_ref), (init_hbm, init_ref), (f_hbm, f_ref))
        )
    ]
    for load in loads:
        load.start()

    lane = lax.broadcasted_iota(jnp.int32, (16, LANES), 1)
    row = lax.broadcasted_iota(jnp.int32, (16, LANES), 0)
    depth = lane % NZ
    half = lane < NZ

    def plane(ref, *index):
        return ref[index].reshape(16, LANES)

    def z_shifts(p):
        before = jnp.where(depth == 0, 0.0, pltpu.roll(p, 1, 1))
        after = jnp.where(depth == NZ - 1, 0.0, pltpu.roll(p, LANES - 1, 1))
        return before, p, after

    def sums_of(sheets, channel):
        sums = []
        for oy in range(3):
            total = None
            for ox in range(3):
                for oz in range(3):
                    place = ox * 9 + oy * 3 + oz
                    if place == 13 or sheets[ox] is None:
                        continue
                    term = st_ref[channel, place - (place > 13)] * sheets[ox][oz]
                    total = term if total is None else total + term
            sums.append(total)
        before, here, after = sums
        above = jnp.where(row == 15, 0.0, pltpu.roll(after, 15, 0))
        below = jnp.where(row == 0, 0.0, pltpu.roll(before, 1, 0))
        return here, jnp.where(half, before + above, below + after)

    def turn(p):
        return pltpu.roll(p, NZ, 1)

    def tile(p):
        return p.reshape(2, 8, LANES)

    def to_sides(buf, halo, send, recv, sem):
        def low():
            return pltpu.make_async_remote_copy(
                buf(0), halo(1), send.at[1, sem], recv.at[1, sem], device_id={"space": s - 1}, device_id_type=MESH
            )

        def high():
            return pltpu.make_async_remote_copy(
                buf(1), halo(0), send.at[0, sem], recv.at[0, sem], device_id={"space": s + 1}, device_id_type=MESH
            )

        def start():
            pl.when(has_low & (s % 2 == 0))(lambda: low().start())
            pl.when(has_high)(lambda: high().start())
            pl.when(has_low & (s % 2 == 1))(lambda: low().start())

        def wait_recv():
            pl.when(has_low)(lambda: high().wait_recv())
            pl.when(has_high)(lambda: low().wait_recv())

        def wait_send():
            pl.when(has_low)(lambda: low().wait_send())
            pl.when(has_high)(lambda: high().wait_send())

        return start, wait_recv, wait_send

    def x_sides(g):
        return to_sides(lambda x: xb.at[:, g, :, pl.ds(2 * x, 2)], lambda x: xh.at[x, :, g], xh_send, xh_recv, g)

    def q_sides():
        return to_sides(lambda x: q.at[:, :, pl.ds(2 * x, 2)], lambda x: qh.at[x], qh_send, qh_recv, 0)

    def a_sides(g):
        return to_sides(lambda x: a.at[:, g, :, pl.ds(2 * x, 2)], lambda x: ah.at[x, :, g], ah_send, ah_recv, g)

    def c_sides(g):
        return to_sides(lambda x: cc.at[g, :, pl.ds(2 * x, 2)], lambda x: ch.at[x, g], ch_send, ch_recv, g)

    def chunk(ref, g, owner):
        return ref.at[g, owner // 4, owner % 4]

    def gather(src, dst, stage, g):
        for owner in partners:
            pltpu.make_async_remote_copy(
                chunk(src, g, owner), dst.at[g, t], s_send.at[stage, g], s_recv.at[stage, g],
                device_id={"tm": owner, "space": other}, device_id_type=MESH,
            ).start()

    def scatter(src, dst, stage, g):
        for to in partners:
            pltpu.make_async_remote_copy(
                src.at[g, to], chunk(dst, g, t), s_send.at[stage, g], s_recv.at[stage, g],
                device_id={"tm": to, "space": other}, device_id_type=MESH,
            ).start()

    def constants(i):
        src = q if i == 0 else ini
        return pltpu.make_async_remote_copy(
            src.at[:, t // 4, t % 4], mine.at[i], mine_send.at[i], mine_recv.at[i],
            device_id={"space": other}, device_id_type=MESH,
        )

    def await_all(stage, g, sem):
        some = r.at[g]
        pltpu.make_async_copy(some, some, sem.at[stage, g]).wait()

    def solve(src, dst, g, first):
        rate = mine[0, g]
        rate = rate * rate
        total, power = src[g, 0], rate
        for n in range(1, groups):
            total = rate * total + src[g, n]
            power = power * rate
        total = wrap_weight * total if first is None else first + wrap_weight * total
        carry = total / (1.0 - wrap_weight * power)
        for n in range(groups):
            dst[g, n] = carry
            if n < groups - 1:
                carry = rate * carry + src[g, n]

    def split(c, _):
        for n in range(2):
            for x in range(2):
                xb[n, c // GC, c % GC, pl.ds(2 * x, 2)] = x_ref[n, c, pl.ds(x, 16, 2), :].reshape(2, 8, LANES)
        return 0

    def rates(c, _):
        g, i = c // GC, c % GC
        for x in range(2):
            gain = damp_ref[c, pl.ds(x, 16, 2), :] + mix_ref[c, c]
            q[g, i, pl.ds(2 * x, 2)] = (1.0 / (1.0 + gain)).reshape(2, 8, LANES)
            ini[g, i, pl.ds(2 * x, 2)] = init_ref[c, pl.ds(x, 16, 2), :].reshape(2, 8, LANES)
        return 0

    loads[0].wait()
    lax.fori_loop(0, NG * GC, split, 0)
    for load in loads[1:5]:
        load.wait()
    lax.fori_loop(0, NG * GC, rates, 0)
    loads[5].wait()
    edges = has_low.astype(jnp.int32) + has_high.astype(jnp.int32)
    pl.semaphore_wait(barrier, len(around + across + flip) + edges)
    greet(second, around + across)

    for g in range(NG):
        x_sides(g)[0]()
    constants(0).start()
    constants(1).start()

    def previous(h):
        some = pl.ds(CUT * h, CUT + h * (NG * GC - 2 * CUT))
        return pltpu.make_async_remote_copy(
            x_ref.at[1, some], prev.at[some], prev_send.at[h], prev_recv.at[h],
            device_id={"tm": t + 1}, device_id_type=MESH,
        )

    pl.when((t < groups - 1) & (y == 0))(lambda: previous(0).start())


    for side, exists in ((0, has_low), (1, has_high)):

        @pl.when(jnp.logical_not(exists))
        def _(side=side):
            xh[side] = jnp.zeros(xh.shape[1:], jnp.float32)
            qh[side] = jnp.zeros(qh.shape[1:], jnp.float32)
            ah[side] = jnp.zeros(ah.shape[1:], jnp.float32)
            ch[side] = jnp.zeros(ch.shape[1:], jnp.float32)

    keep = jnp.where(t < groups - 1, 1.0, 0.0)

    def defects_inside(c, _):
        g, i = c // GC, c % GC
        for n in range(2):
            own = [plane(xb, n, g, i, pl.ds(2 * x, 2)) for x in range(2)]
            moved = [z_shifts(p) for p in own]
            for x in range(2):
                at = pl.ds(2 * x, 2)
                here, turned = sums_of([None, *moved] if x == 0 else [*moved, None], c)
                value = f_ref[n, c, pl.ds(x, 16, 2), :] - own[x] - damp_ref[c, pl.ds(x, 16, 2), :] * own[x] + here
                for d in range(NG * GC):
                    value = value - mix_ref[c, d] * plane(xb, n, d // GC, d % GC, at)
                if n == 1:
                    value = value + plane(xb, 0, g, i, at)
                part[n, g, i, at] = tile(value)
                aside[n, g, i, at] = tile(turned)
        return 0

    pl.semaphore_wait(second, len(around + across))
    greet(third, around)
    pl.when((t < groups - 1) & (y == 1))(lambda: previous(0).start())
    lax.fori_loop(0, NG * GC, defects_inside, 0, unroll=UNROLL)

    def defects(g, _):
        x_sides(g)[1]()

        def channel(i, _):
            c = g * GC + i
            for x in range(2):
                at = pl.ds(2 * x, 2)
                values = []
                for n in range(2):
                    moved = z_shifts(plane(xh, x, n, g, i))
                    here, turned = sums_of([moved, None, None] if x == 0 else [None, None, moved], c)
                    values.append(plane(part, n, g, i, at) + here + turn(plane(aside, n, g, i, at) + turned))
                d0, d1 = values
                rate = plane(q, g, i, at)
                a0 = rate * d0
                a1 = rate * (a0 + d1)
                def_ref[0, c, pl.ds(x, 16, 2), :] = d0
                def_ref[1, c, pl.ds(x, 16, 2), :] = d1
                a[0, g, i, at] = tile(a0)
                a[1, g, i, at] = tile(a1)
                e[g, i, at] = tile(a1 + keep * plane(xb, 1, g, i, at))
            return 0

        lax.fori_loop(0, GC, channel, 0, unroll=UNROLL)
        pl.when(g == 0)(lambda: pl.semaphore_wait(third, len(around)))
        gather(e, r, 0, g)
        return 0

    lax.fori_loop(0, NG, defects, 0)
    for g in range(NG):
        a_sides(g)[0]()
    q_sides()[0]()
    constants(0).wait_recv()
    constants(1).wait_recv()

    def carries(g, _):
        await_all(0, g, s_recv)
        solve(r, co, g, mine[1, g])
        scatter(co, cc, 1, g)
        return 0

    lax.fori_loop(0, NG, carries, 0)

    def first_sweep(g, _):
        await_all(1, g, s_recv)
        c_sides(g)[0]()

        def channel(i, _):
            rate, carry = q[g, i], cc[g, i]
            moved = rate * carry
            u[0, g, i] = a[0, g, i] + moved
            u[1, g, i] = a[1, g, i] + rate * moved
            for n in range(2):
                moved = [z_shifts(plane(u, n, g, i, pl.ds(2 * x, 2))) for x in range(2)]
                for x in range(2):
                    at = pl.ds(2 * x, 2)
                    here, turned = sums_of([None, *moved] if x == 0 else [*moved, None], g * GC + i)
                    part[n, g, i, at] = tile(here)
                    aside[n, g, i, at] = tile(turned)
            return 0

        lax.fori_loop(0, GC, channel, 0, unroll=UNROLL)
        return 0

    lax.fori_loop(0, NG, first_sweep, 0)
    pl.when(t < groups - 1)(lambda: previous(1).start())

    def mixed(c, _):
        g, i = c // GC, c % GC
        for n in range(2):
            value = part[n, g, i]
            for d in range(NG * GC):
                value = value - jnp.where(c == d, 0.0, mix_ref[c, d]) * u[n, d // GC, d % GC]
            part[n, g, i] = value
        return 0

    lax.fori_loop(0, NG * GC, mixed, 0, unroll=UNROLL)
    q_sides()[1]()

    def second_sweep(g, _):
        a_sides(g)[1]()
        c_sides(g)[1]()

        def channel(i, _):
            c = g * GC + i
            for x in range(2):
                at = pl.ds(2 * x, 2)
                rate = plane(qh, x, g, i)
                moved = rate * plane(ch, x, g, i)
                halos = (plane(ah, x, 0, g, i) + moved, plane(ah, x, 1, g, i) + rate * moved)
                values = []
                for n in range(2):
                    moved = z_shifts(halos[n])
                    here, turned = sums_of([moved, None, None] if x == 0 else [None, None, moved], c)
                    values.append(plane(part, n, g, i, at) + here + turn(plane(aside, n, g, i, at) + turned))
                h0, h1 = values
                rate = plane(q, g, i, at)
                v0 = rate * h0
                v1 = rate * (v0 + h1)
                e2[g, i, at] = tile(v1)
                b[0, g, i, at] = tile(plane(xb, 0, g, i, at) + (plane(u, 0, g, i, at) + v0))
                b[1, g, i, at] = tile(plane(xb, 1, g, i, at) + (plane(u, 1, g, i, at) + v1))
            return 0

        lax.fori_loop(0, GC, channel, 0, unroll=UNROLL)
        gather(e2, r2, 2, g)
        return 0

    lax.fori_loop(0, NG, second_sweep, 0)

    def carries_2(g, _):
        await_all(2, g, s_recv)
        solve(r2, co2, g, None)
        scatter(co2, c2, 3, g)
        return 0

    lax.fori_loop(0, NG, carries_2, 0)

    @pl.when(t > 0)
    def _():
        previous(0).wait_recv()
        previous(1).wait_recv()
        def_ref[0] = def_ref[0] + prev[...]

    @pl.when(t == 0)
    def _():
        def_ref[0] = def_ref[0] + init_ref[...]

    def finish(g, _):
        await_all(3, g, s_recv)

        def channel(i, _):
            for x in range(2):
                at = pl.ds(2 * x, 2)
                rate = plane(q, g, i, at)
                moved = rate * plane(c2, g, i, at)
                upd_ref[0, g * GC + i, pl.ds(x, 16, 2), :] = plane(b, 0, g, i, at) + moved
                upd_ref[1, g * GC + i, pl.ds(x, 16, 2), :] = plane(b, 1, g, i, at) + rate * moved
            return 0

        lax.fori_loop(0, GC, channel, 0)
        return 0

    lax.fori_loop(0, NG, finish, 0)

    pl.when(t < groups - 1)(lambda: previous(0).wait_send())
    pl.when(t < groups - 1)(lambda: previous(1).wait_send())
    q_sides()[2]()
    constants(0).wait_send()
    constants(1).wait_send()
    for g in range(NG):
        x_sides(g)[2]()
        a_sides(g)[2]()
        c_sides(g)[2]()
        for stage in range(4):
            await_all(stage, g, s_send)


def rows_of(value):
    lead = value.shape[:-2]
    value = value.reshape(lead + (2, 16, LANES))
    return jnp.swapaxes(value, -3, -2).reshape(lead + (32, LANES))


def planes_of(value):
    lead = value.shape[:-2]
    value = value.reshape(lead + (16, 2, LANES))
    return jnp.swapaxes(value, -3, -2).reshape(lead + (2, 16 * LANES))


def body(forcing, iterate, initial_state, damping, mixing, stencil):
    vmem = pl.BlockSpec(memory_space=pltpu.VMEM)
    hbm = pl.BlockSpec(memory_space=pltpu.HBM)

    def field(*lead):
        return pltpu.VMEM((*lead, NG, GC, 4, 8, LANES), jnp.float32)

    def face(*lead):
        return pltpu.VMEM((*lead, NG, GC, 2, 8, LANES), jnp.float32)

    def rows(*lead):
        return pltpu.VMEM((*lead, NG * GC, 32, LANES), jnp.float32)

    slots = pltpu.VMEM((NG, 16, 8, LANES), jnp.float32)
    dma = pltpu.SemaphoreType.DMA
    results = pl.pallas_call(
        kernel,
        out_shape=rows(2, 2),
        in_specs=[hbm] * 6,
        out_specs=vmem,
        scratch_shapes=[
            rows(2), rows(2), rows(), rows(),
            pltpu.SMEM((NG * GC, NG * GC), jnp.float32), pltpu.SMEM((NG * GC, 26), jnp.float32), dma((6,)),
            pltpu.SemaphoreType.REGULAR, pltpu.SemaphoreType.REGULAR,
            field(2), field(2), pltpu.VMEM((2, NG, 8, LANES), jnp.float32), dma((2,)), dma((2,)),
            field(2), face(2, 2), field(), face(2), field(),
            rows(),
            field(2), face(2, 2),
            field(), slots, slots, field(), face(2),
            field(2), field(2),
            field(), slots, slots, field(),
            dma((2,)), dma((2,)),
            dma((2, NG)), dma((2, NG)),
            dma((2, 1)), dma((2, 1)),
            dma((2, NG)), dma((2, NG)),
            dma((2, NG)), dma((2, NG)),
            dma((4, NG)), dma((4, NG)),
        ],
        compiler_params=pltpu.CompilerParams(
            collective_id=0, has_side_effects=True, vmem_limit_bytes=60 * 1024 * 1024
        ),
    )(rows_of(forcing), rows_of(iterate), rows_of(initial_state), rows_of(damping), mixing, stencil.T)
    return planes_of(results[0]), planes_of(results[1])


def solution(mesh):
    return jax.shard_map(
        body,
        mesh=mesh,
        in_specs=(
            P("tm", None, "space", None),
            P("tm", None, "space", None),
            P(None, "space", None),
            P(None, "space", None),
            P(),
            P(),
        ),
        out_specs=(P("tm", None, "space", None), P("tm", None, "space", None)),
        check_vma=False,
    )
```

```python
import functools

import jax
import jax.numpy as jnp
from jax import lax
from jax.experimental import pallas as pl
from jax.experimental.pallas import tpu as pltpu
from jax.sharding import PartitionSpec as P

NZ = 64
LANES = 128
wrap_weight = 0.05
MESH = pl.DeviceIdType.MESH
NG, GC = 3, 4
UNROLL = 4
CUT = 6


def kernel(
    f_hbm, x_hbm, init_hbm, damp_hbm, mix_hbm, st_hbm,
    out_ref,
    f_ref, x_ref, init_ref, damp_ref, mix_ref, st_ref, load_sem, second, third,
    part, aside, mine, mine_send, mine_recv, xb, xh, q, qh, ini, prev, a, ah, e, r, co, cc, ch, u, b, e2, r2, co2, c2,
    prev_send, prev_recv, xh_send, xh_recv, qh_send, qh_recv, ah_send, ah_recv, ch_send, ch_recv,
    s_send, s_recv,
):
    upd_ref, def_ref = out_ref.at[0], out_ref.at[1]
    groups = lax.axis_size("tm")
    t = lax.axis_index("tm")
    slabs = lax.axis_size("space")
    s = lax.axis_index("space")
    has_low, has_high = s > 0, s < slabs - 1

    other = lax.rem(s + slabs // 2, slabs)
    z, y = t // 2, t % 2
    partners = [
        lax.rem(z + dz, groups // 2) * 2 + (y + dy) % 2 for dz in (4, 3, 5, 2, 6, 1, 7, 0) for dy in range(2)
    ]

    barrier = pltpu.get_barrier_semaphore()
    around = [{"tm": lax.rem(z + dz, groups // 2) * 2 + y} for dz in (2, groups // 2 - 2, 1, groups // 2 - 1)]
    flip = [{"tm": 2 * z + 1 - y}]
    across = [{"tm": 2 * z + dy, "space": other} for dy in range(2)]

    aslant = [
        {"tm": lax.rem(z + dz, groups // 2) * 2 + dy, "space": other} for dz in (1, groups // 2 - 1) for dy in range(2)
    ]

    def greet(sem, devices):
        for device in devices:
            pl.semaphore_signal(sem, inc=1, device_id=device, device_id_type=MESH)

    greet(barrier, around + aslant + across + flip)
    pl.when(has_low)(lambda: greet(barrier, [{"space": s - 1}]))
    pl.when(has_high)(lambda: greet(barrier, [{"space": s + 1}]))
    loads = [
        pltpu.make_async_copy(src, dst, load_sem.at[i])
        for i, (src, dst) in enumerate(
            ((x_hbm, x_ref), (mix_hbm, mix_ref), (st_hbm, st_ref), (damp_hbm, damp_ref), (init_hbm, init_ref), (f_hbm, f_ref))
        )
    ]
    for load in loads:
        load.start()

    lane = lax.broadcasted_iota(jnp.int32, (16, LANES), 1)
    row = lax.broadcasted_iota(jnp.int32, (16, LANES), 0)
    depth = lane % NZ
    half = lane < NZ

    def plane(ref, *index):
        return ref[index].reshape(16, LANES)

    def z_shifts(p):
        before = jnp.where(depth == 0, 0.0, pltpu.roll(p, 1, 1))
        after = jnp.where(depth == NZ - 1, 0.0, pltpu.roll(p, LANES - 1, 1))
        return before, p, after

    def sums_of(sheets, channel):
        sums = []
        for oy in range(3):
            total = None
            for ox in range(3):
                for oz in range(3):
                    place = ox * 9 + oy * 3 + oz
                    if place == 13 or sheets[ox] is None:
                        continue
                    term = st_ref[channel, place - (place > 13)] * sheets[ox][oz]
                    total = term if total is None else total + term
            sums.append(total)
        before, here, after = sums
        above = jnp.where(row == 15, 0.0, pltpu.roll(after, 15, 0))
        below = jnp.where(row == 0, 0.0, pltpu.roll(before, 1, 0))
        return here, jnp.where(half, before + above, below + after)

    def turn(p):
        return pltpu.roll(p, NZ, 1)

    def tile(p):
        return p.reshape(2, 8, LANES)

    def to_sides(buf, halo, send, recv, sem):
        def low():
            return pltpu.make_async_remote_copy(
                buf(0), halo(1), send.at[1, sem], recv.at[1, sem], device_id={"space": s - 1}, device_id_type=MESH
            )

        def high():
            return pltpu.make_async_remote_copy(
                buf(1), halo(0), send.at[0, sem], recv.at[0, sem], device_id={"space": s + 1}, device_id_type=MESH
            )

        def start():
            pl.when(has_low & (s % 2 == 0))(lambda: low().start())
            pl.when(has_high)(lambda: high().start())
            pl.when(has_low & (s % 2 == 1))(lambda: low().start())

        def wait_recv():
            pl.when(has_low)(lambda: high().wait_recv())
            pl.when(has_high)(lambda: low().wait_recv())

        def wait_send():
            pl.when(has_low)(lambda: low().wait_send())
            pl.when(has_high)(lambda: high().wait_send())

        return start, wait_recv, wait_send

    def x_sides(g):
        return to_sides(lambda x: xb.at[:, g, :, pl.ds(2 * x, 2)], lambda x: xh.at[x, :, g], xh_send, xh_recv, g)

    def q_sides():
        return to_sides(lambda x: q.at[:, :, pl.ds(2 * x, 2)], lambda x: qh.at[x], qh_send, qh_recv, 0)

    def a_sides(g):
        return to_sides(lambda x: a.at[:, g, :, pl.ds(2 * x, 2)], lambda x: ah.at[x, :, g], ah_send, ah_recv, g)

    def c_sides(g):
        return to_sides(lambda x: cc.at[g, :, pl.ds(2 * x, 2)], lambda x: ch.at[x, g], ch_send, ch_recv, g)

    def chunk(ref, g, owner):
        return ref.at[g, owner // 4, owner % 4]

    def gather(src, dst, stage, g):
        for owner in partners:
            pltpu.make_async_remote_copy(
                chunk(src, g, owner), dst.at[g, t], s_send.at[stage, g], s_recv.at[stage, g],
                device_id={"tm": owner, "space": other}, device_id_type=MESH,
            ).start()

    def scatter(src, dst, stage, g):
        for to in partners:
            pltpu.make_async_remote_copy(
                src.at[g, to], chunk(dst, g, t), s_send.at[stage, g], s_recv.at[stage, g],
                device_id={"tm": to, "space": other}, device_id_type=MESH,
            ).start()

    def constants(i):
        src = q if i == 0 else ini
        return pltpu.make_async_remote_copy(
            src.at[:, t // 4, t % 4], mine.at[i], mine_send.at[i], mine_recv.at[i],
            device_id={"space": other}, device_id_type=MESH,
        )

    def await_all(stage, g, sem):
        some = r.at[g]
        pltpu.make_async_copy(some, some, sem.at[stage, g]).wait()

    def solve(src, dst, g, first):
        rate = mine[0, g]
        rate = rate * rate
        total, power = src[g, 0], rate
        for n in range(1, groups):
            total = rate * total + src[g, n]
            power = power * rate
        total = wrap_weight * total if first is None else first + wrap_weight * total
        carry = total / (1.0 - wrap_weight * power)
        for n in range(groups):
            dst[g, n] = carry
            if n < groups - 1:
                carry = rate * carry + src[g, n]

    def split(c, _):
        for n in range(2):
            for x in range(2):
                xb[n, c // GC, c % GC, pl.ds(2 * x, 2)] = x_ref[n, c, pl.ds(x, 16, 2), :].reshape(2, 8, LANES)
        return 0

    def rates(c, _):
        g, i = c // GC, c % GC
        for x in range(2):
            gain = damp_ref[c, pl.ds(x, 16, 2), :] + mix_ref[c, c]
            q[g, i, pl.ds(2 * x, 2)] = (1.0 / (1.0 + gain)).reshape(2, 8, LANES)
            ini[g, i, pl.ds(2 * x, 2)] = init_ref[c, pl.ds(x, 16, 2), :].reshape(2, 8, LANES)
        return 0

    loads[0].wait()
    lax.fori_loop(0, NG * GC, split, 0)
    for load in loads[1:5]:
        load.wait()
    lax.fori_loop(0, NG * GC, rates, 0)
    loads[5].wait()
    edges = has_low.astype(jnp.int32) + has_high.astype(jnp.int32)
    pl.semaphore_wait(barrier, len(around + aslant + across + flip) + edges)
    greet(second, around + across)

    for g in range(NG):
        x_sides(g)[0]()
    constants(0).start()
    constants(1).start()

    def previous(h):
        some = pl.ds(CUT * h, CUT + h * (NG * GC - 2 * CUT))
        return pltpu.make_async_remote_copy(
            x_ref.at[1, some], prev.at[some], prev_send.at[h], prev_recv.at[h],
            device_id={"tm": t + 1}, device_id_type=MESH,
        )

    pl.when((t < groups - 1) & (y == 0))(lambda: previous(0).start())


    for side, exists in ((0, has_low), (1, has_high)):

        @pl.when(jnp.logical_not(exists))
        def _(side=side):
            xh[side] = jnp.zeros(xh.shape[1:], jnp.float32)
            qh[side] = jnp.zeros(qh.shape[1:], jnp.float32)
            ah[side] = jnp.zeros(ah.shape[1:], jnp.float32)
            ch[side] = jnp.zeros(ch.shape[1:], jnp.float32)

    keep = jnp.where(t < groups - 1, 1.0, 0.0)

    def defects_inside(c, _):
        g, i = c // GC, c % GC
        for n in range(2):
            own = [plane(xb, n, g, i, pl.ds(2 * x, 2)) for x in range(2)]
            moved = [z_shifts(p) for p in own]
            for x in range(2):
                at = pl.ds(2 * x, 2)
                here, turned = sums_of([None, *moved] if x == 0 else [*moved, None], c)
                value = f_ref[n, c, pl.ds(x, 16, 2), :] - own[x] - damp_ref[c, pl.ds(x, 16, 2), :] * own[x] + here
                for d in range(NG * GC):
                    value = value - mix_ref[c, d] * plane(xb, n, d // GC, d % GC, at)
                if n == 1:
                    value = value + plane(xb, 0, g, i, at)
                part[n, g, i, at] = tile(value)
                aside[n, g, i, at] = tile(turned)
        return 0

    pl.semaphore_wait(second, len(around + across))
    greet(third, around[2:])
    pl.when((t < groups - 1) & (y == 1))(lambda: previous(0).start())
    lax.fori_loop(0, NG * GC, defects_inside, 0, unroll=UNROLL)

    def defects(g, _):
        x_sides(g)[1]()

        def channel(i, _):
            c = g * GC + i
            for x in range(2):
                at = pl.ds(2 * x, 2)
                values = []
                for n in range(2):
                    moved = z_shifts(plane(xh, x, n, g, i))
                    here, turned = sums_of([moved, None, None] if x == 0 else [None, None, moved], c)
                    values.append(plane(part, n, g, i, at) + here + turn(plane(aside, n, g, i, at) + turned))
                d0, d1 = values
                rate = plane(q, g, i, at)
                a0 = rate * d0
                a1 = rate * (a0 + d1)
                def_ref[0, c, pl.ds(x, 16, 2), :] = d0
                def_ref[1, c, pl.ds(x, 16, 2), :] = d1
                a[0, g, i, at] = tile(a0)
                a[1, g, i, at] = tile(a1)
                e[g, i, at] = tile(a1 + keep * plane(xb, 1, g, i, at))
            return 0

        lax.fori_loop(0, GC, channel, 0, unroll=UNROLL)
        pl.when(g == 0)(lambda: pl.semaphore_wait(third, len(around[2:])))
        gather(e, r, 0, g)
        return 0

    lax.fori_loop(0, NG, defects, 0)
    for g in range(NG):
        a_sides(g)[0]()
    q_sides()[0]()
    constants(0).wait_recv()
    constants(1).wait_recv()

    def carries(g, _):
        await_all(0, g, s_recv)
        solve(r, co, g, mine[1, g])
        scatter(co, cc, 1, g)
        return 0

    lax.fori_loop(0, NG, carries, 0)

    def first_sweep(g, _):
        await_all(1, g, s_recv)
        c_sides(g)[0]()

        def channel(i, _):
            rate, carry = q[g, i], cc[g, i]
            moved = rate * carry
            u[0, g, i] = a[0, g, i] + moved
            u[1, g, i] = a[1, g, i] + rate * moved
            for n in range(2):
                moved = [z_shifts(plane(u, n, g, i, pl.ds(2 * x, 2))) for x in range(2)]
                for x in range(2):
                    at = pl.ds(2 * x, 2)
                    here, turned = sums_of([None, *moved] if x == 0 else [*moved, None], g * GC + i)
                    part[n, g, i, at] = tile(here)
                    aside[n, g, i, at] = tile(turned)
            return 0

        lax.fori_loop(0, GC, channel, 0, unroll=UNROLL)
        return 0

    lax.fori_loop(0, NG, first_sweep, 0)
    pl.when(t < groups - 1)(lambda: previous(1).start())

    def mixed(c, _):
        g, i = c // GC, c % GC
        for n in range(2):
            value = part[n, g, i]
            for d in range(NG * GC):
                value = value - jnp.where(c == d, 0.0, mix_ref[c, d]) * u[n, d // GC, d % GC]
            part[n, g, i] = value
        return 0

    lax.fori_loop(0, NG * GC, mixed, 0, unroll=UNROLL)
    q_sides()[1]()

    def second_sweep(g, _):
        a_sides(g)[1]()
        c_sides(g)[1]()

        def channel(i, _):
            c = g * GC + i
            for x in range(2):
                at = pl.ds(2 * x, 2)
                rate = plane(qh, x, g, i)
                moved = rate * plane(ch, x, g, i)
                halos = (plane(ah, x, 0, g, i) + moved, plane(ah, x, 1, g, i) + rate * moved)
                values = []
                for n in range(2):
                    moved = z_shifts(halos[n])
                    here, turned = sums_of([moved, None, None] if x == 0 else [None, None, moved], c)
                    values.append(plane(part, n, g, i, at) + here + turn(plane(aside, n, g, i, at) + turned))
                h0, h1 = values
                rate = plane(q, g, i, at)
                v0 = rate * h0
                v1 = rate * (v0 + h1)
                e2[g, i, at] = tile(v1)
                b[0, g, i, at] = tile(plane(xb, 0, g, i, at) + (plane(u, 0, g, i, at) + v0))
                b[1, g, i, at] = tile(plane(xb, 1, g, i, at) + (plane(u, 1, g, i, at) + v1))
            return 0

        lax.fori_loop(0, GC, channel, 0, unroll=UNROLL)
        gather(e2, r2, 2, g)
        return 0

    lax.fori_loop(0, NG, second_sweep, 0)

    def carries_2(g, _):
        await_all(2, g, s_recv)
        solve(r2, co2, g, None)
        scatter(co2, c2, 3, g)
        return 0

    lax.fori_loop(0, NG, carries_2, 0)

    @pl.when(t > 0)
    def _():
        previous(0).wait_recv()
        previous(1).wait_recv()
        def_ref[0] = def_ref[0] + prev[...]

    @pl.when(t == 0)
    def _():
        def_ref[0] = def_ref[0] + init_ref[...]

    def finish(g, _):
        await_all(3, g, s_recv)

        def channel(i, _):
            for x in range(2):
                at = pl.ds(2 * x, 2)
                rate = plane(q, g, i, at)
                moved = rate * plane(c2, g, i, at)
                upd_ref[0, g * GC + i, pl.ds(x, 16, 2), :] = plane(b, 0, g, i, at) + moved
                upd_ref[1, g * GC + i, pl.ds(x, 16, 2), :] = plane(b, 1, g, i, at) + rate * moved
            return 0

        lax.fori_loop(0, GC, channel, 0)
        return 0

    lax.fori_loop(0, NG, finish, 0)

    pl.when(t < groups - 1)(lambda: previous(0).wait_send())
    pl.when(t < groups - 1)(lambda: previous(1).wait_send())
    q_sides()[2]()
    constants(0).wait_send()
    constants(1).wait_send()
    for g in range(NG):
        x_sides(g)[2]()
        a_sides(g)[2]()
        c_sides(g)[2]()
        for stage in range(4):
            await_all(stage, g, s_send)


def rows_of(value):
    lead = value.shape[:-2]
    value = value.reshape(lead + (2, 16, LANES))
    return jnp.swapaxes(value, -3, -2).reshape(lead + (32, LANES))


def planes_of(value):
    lead = value.shape[:-2]
    value = value.reshape(lead + (16, 2, LANES))
    return jnp.swapaxes(value, -3, -2).reshape(lead + (2, 16 * LANES))


def body(forcing, iterate, initial_state, damping, mixing, stencil):
    vmem = pl.BlockSpec(memory_space=pltpu.VMEM)
    hbm = pl.BlockSpec(memory_space=pltpu.HBM)

    def field(*lead):
        return pltpu.VMEM((*lead, NG, GC, 4, 8, LANES), jnp.float32)

    def face(*lead):
        return pltpu.VMEM((*lead, NG, GC, 2, 8, LANES), jnp.float32)

    def rows(*lead):
        return pltpu.VMEM((*lead, NG * GC, 32, LANES), jnp.float32)

    slots = pltpu.VMEM((NG, 16, 8, LANES), jnp.float32)
    dma = pltpu.SemaphoreType.DMA
    results = pl.pallas_call(
        kernel,
        out_shape=rows(2, 2),
        in_specs=[hbm] * 6,
        out_specs=vmem,
        scratch_shapes=[
            rows(2), rows(2), rows(), rows(),
            pltpu.SMEM((NG * GC, NG * GC), jnp.float32), pltpu.SMEM((NG * GC, 26), jnp.float32), dma((6,)),
            pltpu.SemaphoreType.REGULAR, pltpu.SemaphoreType.REGULAR,
            field(2), field(2), pltpu.VMEM((2, NG, 8, LANES), jnp.float32), dma((2,)), dma((2,)),
            field(2), face(2, 2), field(), face(2), field(),
            rows(),
            field(2), face(2, 2),
            field(), slots, slots, field(), face(2),
            field(2), field(2),
            field(), slots, slots, field(),
            dma((2,)), dma((2,)),
            dma((2, NG)), dma((2, NG)),
            dma((2, 1)), dma((2, 1)),
            dma((2, NG)), dma((2, NG)),
            dma((2, NG)), dma((2, NG)),
            dma((4, NG)), dma((4, NG)),
        ],
        compiler_params=pltpu.CompilerParams(
            collective_id=0, has_side_effects=True, vmem_limit_bytes=60 * 1024 * 1024
        ),
    )(rows_of(forcing), rows_of(iterate), rows_of(initial_state), rows_of(damping), mixing, stencil.T)
    return planes_of(results[0]), planes_of(results[1])


def solution(mesh):
    return jax.shard_map(
        body,
        mesh=mesh,
        in_specs=(
            P("tm", None, "space", None),
            P("tm", None, "space", None),
            P(None, "space", None),
            P(None, "space", None),
            P(),
            P(),
        ),
        out_specs=(P("tm", None, "space", None), P("tm", None, "space", None)),
        check_vma=False,
    )
```
